128 devices in a mesh: dp: 2 (over y_hi), seq: 16 (over y_lo, x, core), tensor: 4 (over z).
Axes of the slice: x: 4, y: 4 (y_hi: 2, y_lo: 2; y = y_hi * 2 + y_lo), z: 4, core: 2. Of those that a mesh axis runs over, the one named last changes fastest.
Arguments:
- queries: bfloat16 [2, 12, 64, 32768], P('dp', 'tensor', None, 'seq'), may hold values from -6 to 6
- key_states: bfloat16 [2, 12, 64, 32768], P('dp', 'tensor', None, 'seq'), may hold values from -6 to 6
- value_states: bfloat16 [2, 12, 64, 32768], P('dp', 'tensor', None, 'seq'), may hold values from -6 to 6
- out_weight: bfloat16 [768, 768], P('tensor'), may hold values from -0.21875 to 0.21875
- grad_output: bfloat16 [2, 32768, 768], P('dp', 'seq'), may hold values from -6 to 6
- phases: int32 [12], P('tensor'), may hold values from 0 to 15
- valid_rows: int32 [2], P('dp'), may hold values from 8192 to 32768
Outputs:
- grad_queries: bfloat16 [2, 12, 64, 32768], P('dp', 'tensor', None, 'seq')
- grad_keys: bfloat16 [2, 12, 64, 32768], P('dp', 'tensor', None, 'seq')
- grad_values: bfloat16 [2, 12, 64, 32768], P('dp', 'tensor', None, 'seq')
- grad_weight: float32 [768, 768], P('tensor')
The draws below stay inside these ranges and needn't reach their ends.
All inputs are finite; a program needn't handle non-finite values.
Results may differ from the reference program's by a relative error of at most 0.017.
Values may be sent and summed in bfloat16 or wider, within the bound.
A program may use at most 128 MiB of HBM per device.

```python
import jax
import jax.numpy as jnp
from jax import lax

D = 768
H = 12
DH = 64
SEG = 1024
RATE = 16
BLK = 32
SLIDES = 2
ROWS = 32768


def head_layout(matrix):
    return matrix.reshape(SLIDES, ROWS, H, DH).transpose(0, 2, 3, 1)


def draw_queries(key, part):
    key = jax.random.fold_in(key, 7)
    base = jax.random.truncated_normal(key, -6.0, 6.0, (SLIDES, ROWS, D)).astype(jnp.float32)
    return head_layout(base).astype(jnp.bfloat16)


def draw_key_states(key, part):
    key = jax.random.fold_in(key, 13)
    base = jax.random.truncated_normal(key, -6.0, 6.0, (SLIDES, ROWS, D)).astype(jnp.float32)
    return head_layout(base).astype(jnp.bfloat16)


def set_ends(values, stream_key, least, high):
    shape = values.shape
    place = [jax.random.randint(jax.random.fold_in(stream_key, axis), (), 0, shape[axis]) for axis in range(len(shape))]
    values = values.at[tuple(place)].set(least)
    longest = shape.index(max(shape))
    place[longest] = (place[longest] + 1) % shape[longest]
    return values.at[tuple(place)].set(high)


def levels(rng, shape, pieces, least, top_value):
    level, own = 1.0, jax.random.fold_in(rng, 6)
    for dim, shards_of in pieces:
        draws = jnp.exp(jax.random.uniform(jax.random.fold_in(own, dim), (shards_of,), jnp.float32, least / len(pieces), top_value / len(pieces)))
        level = level * jnp.repeat(draws, shape[dim] // shards_of).reshape([-1 if axis == dim else 1 for axis in range(len(shape))])
    return level


def scatter_about(own_key, shape, spread, most, shards=(), kind=jnp.bfloat16):
    values = jax.random.normal(own_key, shape, jnp.float32) * spread
    if len(shards) > 0:
        values = levels(own_key, shape, shards, -0.22, 0.18) * values
    return jnp.clip(values, min=-most, max=most).astype(kind)


def setup_inputs(seed: int = 0) -> dict:
    keys = jax.random.split(jax.random.key(seed), 8)
    return {
        "queries": draw_queries(jax.random.fold_in(keys[7], 71), 0),
        "key_states": draw_key_states(jax.random.fold_in(keys[7], 71), 0),
        "value_states": scatter_about(keys[2], (SLIDES, H, DH, ROWS), 1.0, 6.0, ((0, 2), (1, 4), (3, 16))),
        "out_weight": scatter_about(keys[3], (D, D), D ** -0.5, 0.21875, ((0, 4),)),
        "grad_output": scatter_about(keys[4], (SLIDES, ROWS, D), 1.0, 6.0, ((0, 2), (1, 16))),
        "phases": set_ends(jax.random.randint(keys[5], (H,), 0, RATE), jax.random.fold_in(keys[5], 1), 0, RATE - 1).astype(jnp.int32),
        "valid_rows": jax.random.randint(keys[6], (SLIDES,), ROWS // 4, ROWS + 1).astype(jnp.int32),
    }


NEGATIVE = -1e30


def select_rows(matrix, head_phase):
    row_count, col_count = matrix.shape
    blocks = matrix.reshape(row_count // (RATE * BLK), RATE, BLK, col_count)
    picked = lax.dynamic_index_in_dim(blocks, head_phase, 1, keepdims=False)
    return picked.reshape(row_count // RATE, col_count)


def place_rows(full_rows, picked, head_phase):
    row_count, col_count = full_rows.shape
    blocks = full_rows.reshape(row_count // (RATE * BLK), RATE, BLK, col_count)
    inserted = picked.reshape(row_count // (RATE * BLK), 1, BLK, col_count)
    return lax.dynamic_update_slice_in_dim(blocks, inserted, head_phase, 1).reshape(row_count, col_count)


def product(form, left, right):
    return jnp.einsum(form, left.astype(jnp.float32), right.astype(jnp.float32), precision=lax.Precision.HIGHEST)


def level_forward(query_in, key_in, value_in, allowed):
    score_scale = query_in.shape[-1] ** -0.5
    scores = product("...id,...jd->...ij", query_in, key_in) * score_scale
    scores = jnp.where(allowed, scores, NEGATIVE)
    row_max = jnp.max(scores, axis=-1, keepdims=True)
    lse = row_max + jnp.log(jnp.sum(jnp.exp(scores - row_max), axis=-1, keepdims=True))
    probs = jnp.exp(scores - lse).astype(jnp.bfloat16)
    output = product("...ij,...jd->...id", probs, value_in)
    return output, lse[..., 0], probs


def level_backward(query_in, key_in, value_in, probs, output, dout, dlse):
    score_scale = query_in.shape[-1] ** -0.5
    delta = jnp.sum(dout.astype(jnp.float32) * output, axis=-1)
    prob_grad = product("...id,...jd->...ij", dout, value_in)
    score_grad = (probs.astype(jnp.float32) * (prob_grad + (dlse - delta)[..., None])).astype(jnp.bfloat16)
    query_grad = product("...ij,...jd->...id", score_grad, key_in) * score_scale
    key_grad = product("...ij,...id->...jd", score_grad, query_in) * score_scale
    value_grad = product("...ij,...id->...jd", probs, dout)
    return query_grad, key_grad, value_grad


def dilated_head(query_in, key_in, value_in, cotangent, head_phase, allowed_far):
    row_count, head_size = query_in.shape
    segments = row_count // SEG

    def cut(matrix):
        return matrix.reshape(segments, SEG, head_size)

    near_out, near_lse, near_probs = level_forward(cut(query_in), cut(key_in), cut(value_in), True)
    near_out = near_out.reshape(row_count, head_size)
    near_lse = near_lse.reshape(row_count, 1)
    query_pick = select_rows(query_in, head_phase)
    key_pick = select_rows(key_in, head_phase)
    value_pick = select_rows(value_in, head_phase)
    far_out, far_lse, far_probs = level_forward(query_pick, key_pick, value_pick, allowed_far)
    near_pick = select_rows(near_out, head_phase)
    mixing = jax.nn.sigmoid(far_lse - select_rows(near_lse, head_phase)[:, 0])
    combined = place_rows(near_out, near_pick + mixing[:, None] * (far_out - near_pick), head_phase)
    grad_full = cotangent.astype(jnp.float32)
    grad_pick = select_rows(grad_full, head_phase)
    mix_grad = jnp.sum(grad_pick * (far_out - near_pick), axis=1)
    far_dlse = mix_grad * mixing * (1.0 - mixing)
    far_dout = (mixing[:, None] * grad_pick).astype(jnp.bfloat16)
    near_dout = place_rows(grad_full, (1.0 - mixing)[:, None] * grad_pick, head_phase).astype(jnp.bfloat16)
    near_dlse = place_rows(jnp.zeros((row_count, 1), jnp.float32), -far_dlse[:, None], head_phase)
    near_q, near_k, near_v = level_backward(cut(query_in), cut(key_in), cut(value_in), near_probs, cut(near_out), cut(near_dout), near_dlse.reshape(segments, SEG))
    far_q, far_k, far_v = level_backward(query_pick, key_pick, value_pick, far_probs, far_out, far_dout, far_dlse)
    empty = jnp.zeros((row_count, head_size), jnp.float32)
    query_grad = near_q.reshape(row_count, head_size) + place_rows(empty, far_q, head_phase)
    key_grad = near_k.reshape(row_count, head_size) + place_rows(empty, far_k, head_phase)
    value_grad = near_v.reshape(row_count, head_size) + place_rows(empty, far_v, head_phase)
    return combined, query_grad, key_grad, value_grad


def reference(queries, key_states, value_states, out_weight, grad_output, phases, valid_rows):
    slide_count, head_count, head_size, row_count = queries.shape
    width_all = head_count * head_size
    grad_weight = jnp.zeros((width_all, width_all), jnp.float32)
    query_list, key_list, value_list = [], [], []
    for slide_index in range(slide_count):
        grad_attn = jnp.dot(grad_output[slide_index], out_weight.T, preferred_element_type=jnp.float32).astype(jnp.bfloat16)
        valid_count = valid_rows[slide_index]

        def head_rows(stacked):
            return stacked.transpose(0, 2, 1)

        def split_heads(matrix):
            return matrix.reshape(row_count, head_count, head_size).transpose(1, 0, 2)

        def merge_heads(stacked):
            return stacked.transpose(1, 0, 2).reshape(row_count, width_all)

        def one_head(head_items):
            query_rows, key_rows, value_rows, cotangent, head_phase = head_items
            far_index = select_rows(jnp.arange(row_count, dtype=jnp.int32)[:, None], head_phase)[:, 0]
            allowed_far = (far_index < valid_count)[None, :]
            return dilated_head(query_rows, key_rows, value_rows, cotangent, head_phase, allowed_far)

        combined, query_grad, key_grad, value_grad = lax.map(one_head, (head_rows(queries[slide_index]), head_rows(key_states[slide_index]), head_rows(value_states[slide_index]), split_heads(grad_attn), phases))
        attn_out = merge_heads(combined).astype(jnp.bfloat16)
        grad_weight = grad_weight + jnp.dot(attn_out.T, grad_output[slide_index], preferred_element_type=jnp.float32)
        query_list.append(query_grad.transpose(0, 2, 1))
        key_list.append(key_grad.transpose(0, 2, 1))
        value_list.append(value_grad.transpose(0, 2, 1))
    return (jnp.stack(query_list).astype(jnp.bfloat16), jnp.stack(key_list).astype(jnp.bfloat16), jnp.stack(value_list).astype(jnp.bfloat16), grad_weight)
```

```python
import jax
import jax.numpy as jnp
from jax import lax
from jax.experimental import pallas as pl
from jax.experimental.pallas import tpu as pltpu
from jax.sharding import PartitionSpec as P

F32 = jnp.float32
BF16 = jnp.bfloat16
SEG = 1024
RATE = 16
BLK = 32
HEADS = 3
DH = 64
ROWS = 2048
SUB = ROWS // RATE
D = 768
PEERS = 16
SPAN = PEERS * SUB
SCALE = 0.125
LOG2E = 1.4426950408889634
QD_ROWS = 144
MESH = pl.DeviceIdType.MESH


def nn(a, b):
    return jnp.dot(a, b, preferred_element_type=F32)


def nt(a, b):
    return lax.dot_general(a, b, (((1,), (1,)), ((), ())), preferred_element_type=F32)


def hi_lo(x):
    hi = x.astype(BF16)
    return hi, (x - hi.astype(F32)).astype(BF16)


def split3(x):
    hi = x.astype(BF16)
    rest = x - hi.astype(F32)
    mid = rest.astype(BF16)
    return hi, mid, (rest - mid.astype(F32)).astype(BF16)


def lanes(n=SUB):
    return lax.broadcasted_iota(jnp.int32, (1, n), 1)


def turn(x, groups):
    groups = groups % 4
    return x if groups == 0 else pltpu.roll(x, groups * 32, 1)


def choose(options, which):
    out = options[0]
    for n in range(1, len(options)):
        out = jnp.where(which == n, options[n], out)
    return out


def pick(load, phase):
    chunk = jnp.full((1, SUB), phase >> 2, jnp.int32)
    part = jnp.full((1, SUB), phase & 3, jnp.int32)
    group = lanes() >> 5
    out = None
    for b in range(4):
        x = choose([load(b * 512 + n * 128).astype(F32) for n in range(4)], chunk)
        x = choose([turn(x, b - n) for n in range(4)], part)
        out = x if b == 0 else jnp.where(group == b, x, out)
    return out


def place_parts(x, phase):
    part = jnp.full((1, SUB), phase & 3, jnp.int32)
    turned = [turn(x, n) for n in range(4)]
    return [choose([turned[(n - b) % 4] for n in range(4)], part) for b in range(4)]


def place_mask(phase, c):
    want = jnp.where((phase >> 2) == (c % 4), phase & 3, -1)
    return (lanes() >> 5) == want


def kernel(
    phases, valid, q_hbm, k_hbm, v_hbm, w_hbm, go_hbm,
    dq_hbm, dk_hbm, dv_hbm, gw_hbm,
    q_s, k_s, v_s, w_s, go_s, g_s, e_s, ds_s, on_s, st_s, nd_s, at_s,
    kv_buf, qd_buf, fe_s, fq_s, fr_s,
    aq_s, ak_s, av_s, oq_s, ok_s, ov_s,
    gw_s, a_send, a_recv, half_s, b_send, b_recv, c_buf, d_buf,
    in_sem, out_sem, kv_send, kv_recv, qd_send, qd_recv, pair_send, pair_recv,
    a_sem, b_ss, b_rs, c_ss, c_rs, d_ss, d_rs,
):
    dp, sq, tz = lax.axis_index("dp"), lax.axis_index("seq"), lax.axis_index("tensor")
    y, x, core = sq // 8, (sq % 8) // 2, sq % 2
    yx = sq // 2
    yg = dp * 2 + y

    copies = [
        pltpu.make_async_copy(k_hbm.at[0], k_s, in_sem.at[0]),
        pltpu.make_async_copy(v_hbm.at[0], v_s, in_sem.at[1]),
        pltpu.make_async_copy(q_hbm.at[0], q_s, in_sem.at[2]),
        pltpu.make_async_copy(w_hbm, w_s, in_sem.at[3]),
        pltpu.make_async_copy(go_hbm.at[0], go_s, in_sem.at[4]),
    ]
    for c in copies:
        c.start()

    def at_yx(k):
        yy, xx = (y + k // 4) % 2, (x + k % 4) % 4
        return yy * 4 + xx

    def from_yx(k):
        yy, xx = (y + 2 - k // 4) % 2, (x + 4 - k % 4) % 4
        return yy * 4 + xx

    same_core = [(dp, at_yx(k) * 2 + core, tz) for k in range(1, 8)]
    sibling = (dp, yx * 2 + 1 - core, tz)
    other_core = [(dp, (y * 4 + (x + k) % 4) * 2 + 1 - core, tz) for k in range(1, 4)]
    y_peers = []
    for k in range(1, 4):
        there = (yg + k) % 4
        y_peers.append((there // 2, (there % 2) * 8 + x * 2 + core, tz))
    barrier = pltpu.get_barrier_semaphore()
    dp_peers = [(1 - dp, yy * 8 + x * 2 + core, tz) for yy in range(2)]
    greet = same_core + [sibling] + other_core + dp_peers
    for peer in greet:
        pl.semaphore_signal(barrier, inc=1, device_id=peer, device_id_type=MESH)

    for c in copies[:2]:
        c.wait()
    for h in range(HEADS):
        ph = phases[h]
        kv_buf[core, yx, h, 0:DH, :] = pick(lambda o: k_s[h, :, pl.ds(o, 128)], ph).astype(BF16)
        kv_buf[core, yx, h, DH:2 * DH, :] = pick(lambda o: v_s[h, :, pl.ds(o, 128)], ph).astype(BF16)
    pl.semaphore_wait(barrier, len(greet))

    def gather(buf, ss, rs):
        sends, recvs = [], []
        for k in range(1, 8):
            mine = buf.at[core, yx]
            sends.append(pltpu.make_async_remote_copy(
                mine, mine, ss.at[k - 1], rs.at[k - 1], device_id=same_core[k - 1], device_id_type=MESH))
            theirs = buf.at[core, from_yx(k)]
            recvs.append(pltpu.make_async_remote_copy(
                theirs, theirs, ss.at[k - 1], rs.at[k - 1], device_id=same_core[k - 1], device_id_type=MESH))
        return sends, recvs

    def to_pair(buf, i):
        out = pltpu.make_async_remote_copy(
            buf.at[core], buf.at[core], pair_send.at[i], pair_recv.at[i], device_id=sibling, device_id_type=MESH)
        back = pltpu.make_async_remote_copy(
            buf.at[1 - core], buf.at[1 - core], pair_send.at[i], pair_recv.at[i], device_id=sibling, device_id_type=MESH)
        return out, back

    kv_out, kv_in = gather(kv_buf, kv_send, kv_recv)
    for c in kv_out:
        c.start()

    copies[2].wait()
    for h in range(HEADS):
        qd_buf[core, yx, h, 0:DH, :] = pick(lambda o: q_s[h, :, pl.ds(o, 128)], phases[h]).astype(BF16)

    def near_forward(u, carry):
        h, off = u // 2, pl.multiple_of((u % 2) * SEG, SEG)
        rows = pl.ds(off, SEG)
        k_t, v_t = k_s[h, :, rows], v_s[h, :, rows]
        qh, ql = hi_lo(q_s[h, :, rows].astype(F32) * (SCALE * LOG2E))
        kk = jnp.concatenate([k_t, k_t], 0).T
        s = nn(kk, jnp.concatenate([qh, ql], 0))
        m = jnp.max(s, axis=0, keepdims=True)
        e = jnp.exp2(s - m).astype(BF16)
        e_s[u] = e
        o = nn(jnp.concatenate([v_t, jnp.ones((16, SEG), BF16)], 0), e)
        total = o[DH:DH + 1]
        r = 1.0 / total
        on_s[h, :, rows] = o[:DH] * r
        st_s[h, 0:1, rows] = r
        st_s[h, 1:2, rows] = m + jnp.log2(total)
        return carry

    lax.fori_loop(0, 2 * HEADS, near_forward, 0)

    for c in kv_in:
        c.wait_recv()
    kv_pair, kv_back = to_pair(kv_buf, 0)
    kv_pair.start()
    copies[3].wait()
    copies[4].wait()
    g_s[...] = nt(w_s[...], go_s[...]).astype(BF16).reshape(HEADS, DH, ROWS)
    kv_back.wait_recv()

    key_index = lanes(SPAN)

    def all_cols(buf, h, lo, hi):
        return jnp.concatenate([buf[n % 2, n // 2, h, lo:hi, :] for n in range(PEERS)], 1)

    def far_forward(h, carry):
        ph = phases[h]
        k_t, v_t = all_cols(kv_buf, h, 0, DH), all_cols(kv_buf, h, DH, 2 * DH)
        q_t = qd_buf[core, yx, h, 0:DH, :].astype(F32) * (SCALE * LOG2E)
        hi = q_t.astype(BF16).astype(F32)
        lhs = jnp.concatenate([hi, q_t - hi], 0).T.astype(BF16)
        s = nn(lhs, jnp.concatenate([k_t, k_t], 0))
        row = (key_index >> 5) * (RATE * BLK) + ph * BLK + (key_index & 31)
        s = jnp.where(row < valid[0], s, -1e30)
        m = jnp.max(s, axis=1, keepdims=True)
        e = jnp.exp2(s - m).astype(BF16)
        fe_s[h] = e
        o = nt(e, jnp.concatenate([v_t, jnp.ones((16, SPAN), BF16)], 0))
        total = o[:, DH:DH + 1]
        r = 1.0 / total
        packed = jnp.concatenate(
            [o[:, :DH] * r, jnp.broadcast_to(m + jnp.log2(total), (SUB, 32)), jnp.broadcast_to(r, (SUB, 32))], 1).T
        far_out, far_lse, far_r = packed[0:DH], packed[DH:DH + 1], packed[96:97]
        near_out = pick(lambda o: on_s[h, :, pl.ds(o, 128)], ph)
        near_lse = pick(lambda o: st_s[h, :, pl.ds(o, 128)], ph)[1:2]
        g = pick(lambda o: g_s[h, :, pl.ds(o, 128)], ph)
        mixing = 1.0 / (1.0 + jnp.exp2(near_lse - far_lse))
        rest = 1.0 / (1.0 + jnp.exp2(far_lse - near_lse))
        diff = far_out - near_out
        comb = near_out + mixing * diff
        far_dlse = jnp.sum(g * diff, axis=0, keepdims=True) * mixing * rest
        far_dout = (mixing * g).astype(BF16)
        fd = far_dout.astype(F32)
        term = far_dlse - jnp.sum(fd * far_out, axis=0, keepdims=True)
        qd_buf[core, yx, h, DH:2 * DH, :] = far_dout
        qd_buf[core, yx, h, 2 * DH:QD_ROWS, :] = jnp.concatenate(
            [*split3(-far_lse), *split3(term), jnp.zeros((10, SUB), BF16)], 0)
        scaled = (fd * far_r).astype(BF16).astype(F32)
        term_r = far_dlse * far_r - jnp.sum(scaled * far_out, axis=0, keepdims=True)
        fr_s[h, 0:DH, :] = scaled
        fr_s[h, DH:DH + 8, :] = jnp.broadcast_to(term_r, (8, SUB))
        stack = jnp.concatenate([comb, rest, -far_dlse, jnp.zeros((6, SUB), F32)], 0)
        parts = place_parts(stack, ph)
        for c in range(16):
            cols = pl.ds(c * 128, 128)
            mask = place_mask(ph, c)
            part = parts[c // 4]
            near = on_s[h, :, cols]
            at_s[h, :, cols] = jnp.where(mask, part[:DH], near).astype(BF16)
            factor = jnp.where(mask, part[DH:DH + 1], 1.0)
            dlse = jnp.where(mask, part[DH + 1:DH + 2], 0.0)
            rr = st_s[h, 0:1, cols]
            nd = (g_s[h, :, cols].astype(F32) * factor).astype(BF16).astype(F32)
            nd = (nd * rr).astype(BF16)
            nd_s[h, :, cols] = nd
            st_s[h, 2:3, cols] = dlse * rr - jnp.sum(nd.astype(F32) * near, axis=0, keepdims=True)
        return carry

    lax.fori_loop(0, HEADS, far_forward, 0)

    for c in kv_out:
        c.wait_send()
    kv_pair.wait_send()
    qd_out, qd_in = gather(qd_buf, qd_send, qd_recv)
    for c in qd_out:
        c.start()

    gw_s[...] = nn(at_s[...].reshape(HEADS * DH, ROWS), go_s[...])
    half = HEADS * DH // 2
    a_send[...] = gw_s[pl.ds(pl.multiple_of((1 - core) * half, 32), half), :].astype(BF16)
    a_copy = pltpu.make_async_remote_copy(a_send, a_recv, a_sem.at[0], a_sem.at[1], device_id=sibling, device_id_type=MESH)
    a_copy.start()

    def far_backward_q(h, carry):
        k_t, v_t = all_cols(kv_buf, h, 0, DH), all_cols(kv_buf, h, DH, 2 * DH)
        d = fr_s[h]
        term = d[DH:DH + 1]
        term_hi = term.astype(BF16).astype(F32)
        left = jnp.concatenate([d[:DH], term_hi, term - term_hi, jnp.zeros((62, SUB), F32)], 0).T.astype(BF16)
        ones = jnp.concatenate([jnp.ones((2, SPAN), BF16), jnp.zeros((62, SPAN), BF16)], 0)
        dprob = nn(left, jnp.concatenate([v_t, ones], 0))
        dscore = dprob.astype(BF16) * fe_s[h]
        fq_s[h] = nt(dscore, k_t).T * SCALE
        return carry

    lax.fori_loop(0, HEADS, far_backward_q, 0)

    quarter, wide = half // 2, D // 2
    b_out, b_in = [], []
    for k in range(1, 4):
        b_out.append(pltpu.make_async_remote_copy(
            b_send.at[(x + k) % 4], b_recv.at[x], b_ss.at[k - 1], b_rs.at[k - 1],
            device_id=same_core[k - 1], device_id_type=MESH))
        b_in.append(pltpu.make_async_remote_copy(
            b_send.at[(x + k) % 4], b_recv.at[(x + 4 - k) % 4], b_ss.at[k - 1], b_rs.at[k - 1],
            device_id=same_core[k - 1], device_id_type=MESH))
    c_out, c_in = [], []
    for k in range(1, 4):
        c_out.append(pltpu.make_async_remote_copy(
            c_buf.at[yg], c_buf.at[yg], c_ss.at[k - 1], c_rs.at[k - 1], device_id=y_peers[k - 1], device_id_type=MESH))
        there = (yg + 4 - k) % 4
        c_in.append(pltpu.make_async_remote_copy(
            c_buf.at[there], c_buf.at[there], c_ss.at[k - 1], c_rs.at[k - 1], device_id=y_peers[k - 1], device_id_type=MESH))
    d_out, d_in = [], []
    d_peers = [same_core[k - 1] for k in range(1, 4)] + [sibling] + other_core
    for k in range(1, 8):
        here = d_buf.at[core, x]
        d_out.append(pltpu.make_async_remote_copy(
            here, here, d_ss.at[k - 1], d_rs.at[k - 1], device_id=d_peers[k - 1], device_id_type=MESH))
        theirs = d_buf.at[core if k < 4 else 1 - core, (x + 4 - k % 4) % 4]
        d_in.append(pltpu.make_async_remote_copy(
            theirs, theirs, d_ss.at[k - 1], d_rs.at[k - 1], device_id=d_peers[k - 1], device_id_type=MESH))
    qd_pair, qd_back = to_pair(qd_buf, 1)

    def near_backward(u, carry):
        h, off = u // 2, pl.multiple_of((u % 2) * SEG, SEG)
        rows = pl.ds(off, SEG)
        q_t, k_t, v_t, gh = q_s[h, :, rows], k_s[h, :, rows], v_s[h, :, rows], nd_s[h, :, rows]
        th, tl = hi_lo(st_s[h, 2:3, rows])
        gg = jnp.concatenate([gh, jnp.concatenate([th, tl, jnp.zeros((14, SEG), BF16)], 0)], 0)
        vv = jnp.concatenate([v_t, jnp.ones((2, SEG), BF16), jnp.zeros((14, SEG), BF16)], 0).T
        for ib in range(2):
            cols = slice(ib * 512, ib * 512 + 512)
            dprob = nn(vv, gg[:, cols])
            ds = dprob.astype(BF16) * e_s[u, :, cols]
            ds_s[:, cols] = ds
            aq_s[h, :, pl.ds(pl.multiple_of(off + ib * 512, 512), 512)] = nn(k_t, ds) * SCALE
        for jb in range(2):
            cols = slice(jb * 512, jb * 512 + 512)
            out_cols = pl.ds(pl.multiple_of(off + jb * 512, 512), 512)
            ak_s[h, :, out_cols] = nt(ds_s[cols, :], q_t).T * SCALE
            av_s[h, :, out_cols] = nt(e_s[u, cols, :], gh).T

        @pl.when(u == 0)
        def _():
            a_copy.wait()
            mine = gw_s[pl.ds(pl.multiple_of(core * half, 32), half), :]
            half_s[...] = mine + a_recv[...].astype(F32)
            for t in range(4):
                b_send[t] = half_s[(t // 2) * quarter:(t // 2 + 1) * quarter, (t % 2) * wide:(t % 2 + 1) * wide].astype(BF16)
            for c in b_out:
                c.start()

        @pl.when(u == 2)
        def _():
            for c in b_in:
                c.wait_recv()
            b_recv[x] = b_send[x]
            total = b_recv[0].astype(F32)
            for t in range(1, 4):
                total = total + b_recv[t].astype(F32)
            c_buf[yg] = total.astype(BF16)
            for c in c_out:
                c.start()

        @pl.when(u == 3)
        def _():
            for c in c_in:
                c.wait_recv()
            total = c_buf[0].astype(F32)
            for t in range(1, 4):
                total = total + c_buf[t].astype(F32)
            d_buf[core, x] = total.astype(BF16)
            for c in d_out:
                c.start()

        @pl.when(u == 4)
        def _():
            for c in qd_in:
                c.wait_recv()
            qd_pair.start()

        return carry

    lax.fori_loop(0, 2 * HEADS, near_backward, 0)
    qd_back.wait_recv()

    def outs(h):
        return [
            pltpu.make_async_copy(oq_s.at[h], dq_hbm.at[0, h], out_sem.at[0, h]),
            pltpu.make_async_copy(ok_s.at[h], dk_hbm.at[0, h], out_sem.at[1, h]),
            pltpu.make_async_copy(ov_s.at[h], dv_hbm.at[0, h], out_sem.at[2, h]),
        ]

    def far_backward_kv(h, carry):
        ph = phases[h]
        q_t, do_t = all_cols(qd_buf, h, 0, DH), all_cols(qd_buf, h, DH, 2 * DH)
        stats = all_cols(qd_buf, h, 2 * DH, QD_ROWS)
        own_k = kv_buf[core, yx, h, 0:DH, :].astype(F32) * (SCALE * LOG2E)
        own_v = kv_buf[core, yx, h, DH:2 * DH, :].astype(F32)
        hi = own_k.astype(BF16).astype(F32)
        index = lax.broadcasted_iota(jnp.int32, (16, SUB), 0)
        first = jnp.where(index < 3, 1.0, 0.0)
        second = jnp.where((index >= 3) & (index < 6), 1.0, 0.0)
        zeros = jnp.zeros((48, SUB), F32)
        left_s = jnp.concatenate([hi, own_k - hi, first, zeros, zeros, jnp.zeros((16, SUB), F32)], 0).T.astype(BF16)
        s = nn(left_s[:, :QD_ROWS], jnp.concatenate([q_t, q_t, stats], 0))
        j = lax.broadcasted_iota(jnp.int32, (SUB, 1), 0)
        row = sq * ROWS + (j >> 5) * (RATE * BLK) + ph * BLK + (j & 31)
        probs = jnp.where(row < valid[0], jnp.exp2(s), 0.0).astype(BF16)
        left_d = jnp.concatenate([own_v, second, zeros], 0).T.astype(BF16)
        dprob = nn(left_d[:, :DH + 16], jnp.concatenate([do_t, stats], 0))
        dscore = dprob.astype(BF16) * probs
        both = jnp.concatenate([nt(dscore, q_t) * SCALE, nt(probs, do_t)], 1).T
        parts_k, parts_v = place_parts(both[:DH], ph), place_parts(both[DH:], ph)
        parts_q = place_parts(fq_s[h], ph)
        for c in range(16):
            cols = pl.ds(c * 128, 128)
            mask = place_mask(ph, c)
            for out, near, parts in ((oq_s, aq_s, parts_q), (ok_s, ak_s, parts_k), (ov_s, av_s, parts_v)):
                out[h, :, cols] = (near[h, :, cols] + jnp.where(mask, parts[c // 4], 0.0)).astype(BF16)
        for c in outs(h):
            c.start()
        return carry

    lax.fori_loop(0, HEADS, far_backward_kv, 0)

    for c in d_in:
        c.wait_recv()
    for cc in range(2):
        for t in range(4):
            gw_s[cc * half + (t // 2) * quarter:cc * half + (t // 2 + 1) * quarter, (t % 2) * wide:(t % 2 + 1) * wide] = (
                d_buf[cc, t].astype(F32))
    gw_copy = pltpu.make_async_copy(gw_s, gw_hbm, in_sem.at[0])
    gw_copy.start()
    for c in qd_out + [qd_pair] + b_out + c_out + d_out:
        c.wait_send()
    for h in range(HEADS):
        for c in outs(h):
            c.wait()
    gw_copy.wait()


def shards(queries, key_states, value_states, out_weight, grad_output, phases, valid_rows):
    big = lambda dtype: pltpu.VMEM((HEADS, DH, ROWS), dtype)
    dma = pltpu.SemaphoreType.DMA
    any_spec = pl.BlockSpec(memory_space=pl.ANY)
    smem = pl.BlockSpec(memory_space=pltpu.SMEM)
    chunk = (HEADS * DH // 4, D // 2)
    state = jax.ShapeDtypeStruct(queries.shape, BF16)
    return pl.pallas_call(
        kernel,
        out_shape=[state, state, state, jax.ShapeDtypeStruct((HEADS * DH, D), F32)],
        in_specs=[smem, smem] + [any_spec] * 5,
        out_specs=[any_spec] * 4,
        scratch_shapes=[
            big(BF16), big(BF16), big(BF16),
            pltpu.VMEM((HEADS * DH, D), BF16), pltpu.VMEM((ROWS, D), BF16),
            big(BF16),
            pltpu.VMEM((2 * HEADS, SEG, SEG), BF16), pltpu.VMEM((SEG, SEG), BF16),
            big(F32), pltpu.VMEM((HEADS, 8, ROWS), F32), big(BF16), big(BF16),
            pltpu.VMEM((2, 8, HEADS, 2 * DH, SUB), BF16), pltpu.VMEM((2, 8, HEADS, QD_ROWS, SUB), BF16),
            pltpu.VMEM((HEADS, SUB, SPAN), BF16), pltpu.VMEM((HEADS, DH, SUB), F32), pltpu.VMEM((HEADS, DH + 8, SUB), F32),
            big(F32), big(F32), big(F32), big(BF16), big(BF16), big(BF16),
            pltpu.VMEM((HEADS * DH, D), F32),
            pltpu.VMEM((HEADS * DH // 2, D), BF16), pltpu.VMEM((HEADS * DH // 2, D), BF16),
            pltpu.VMEM((HEADS * DH // 2, D), F32),
            pltpu.VMEM((4, *chunk), BF16), pltpu.VMEM((4, *chunk), BF16), pltpu.VMEM((4, *chunk), BF16),
            pltpu.VMEM((2, 4, *chunk), BF16),
            dma((5,)), dma((3, HEADS)), dma((7,)), dma((7,)), dma((7,)), dma((7,)), dma((2,)), dma((2,)),
            dma((2,)), dma((3,)), dma((3,)), dma((3,)), dma((3,)), dma((7,)), dma((7,)),
        ],
        compiler_params=pltpu.CompilerParams(
            collective_id=0, has_side_effects=True, vmem_limit_bytes=58 << 20),
        name="dilated_backward",
    )(phases, valid_rows, queries, key_states, value_states, out_weight, grad_output)


def solution(mesh):
    heads = P("dp", "tensor", None, "seq")
    return jax.shard_map(
        shards, mesh=mesh,
        in_specs=(heads, heads, heads, P("tensor", None), P("dp", "seq", None), P("tensor"), P("dp")),
        out_specs=(heads, heads, heads, P("tensor", None)),
        check_vma=False,
    )
```

```python
import jax
import jax.numpy as jnp
from jax import lax
from jax.experimental import pallas as pl
from jax.experimental.pallas import tpu as pltpu
from jax.sharding import PartitionSpec as P

F32 = jnp.float32
BF16 = jnp.bfloat16
SEG = 1024
RATE = 16
BLK = 32
HEADS = 3
DH = 64
ROWS = 2048
SUB = ROWS // RATE
D = 768
PEERS = 16
SPAN = PEERS * SUB
SCALE = 0.125
LOG2E = 1.4426950408889634
DO_ROWS = 80
QD_ROWS = DH + DO_ROWS
MESH = pl.DeviceIdType.MESH


def nn(a, b):
    return jnp.dot(a, b, preferred_element_type=F32)


def nt(a, b):
    return lax.dot_general(a, b, (((1,), (1,)), ((), ())), preferred_element_type=F32)


def hi_lo(x):
    hi = x.astype(BF16)
    return hi, (x - hi.astype(F32)).astype(BF16)


def split3(x):
    hi = x.astype(BF16)
    rest = x - hi.astype(F32)
    mid = rest.astype(BF16)
    return hi, mid, (rest - mid.astype(F32)).astype(BF16)


def lanes(n=SUB):
    return lax.broadcasted_iota(jnp.int32, (1, n), 1)


def turn(x, groups):
    groups = groups % 4
    return x if groups == 0 else pltpu.roll(x, groups * 32, 1)


def choose(options, which):
    out = options[0]
    for n in range(1, len(options)):
        out = jnp.where(which == n, options[n], out)
    return out


def pick(load, phase):
    chunk = jnp.full((1, SUB), phase >> 2, jnp.int32)
    part = jnp.full((1, SUB), phase & 3, jnp.int32)
    group = lanes() >> 5
    out = None
    for b in range(4):
        x = choose([load(b * 512 + n * 128).astype(F32) for n in range(4)], chunk)
        x = choose([turn(x, b - n) for n in range(4)], part)
        out = x if b == 0 else jnp.where(group == b, x, out)
    return out


def place_parts(x, phase):
    part = jnp.full((1, SUB), phase & 3, jnp.int32)
    turned = [turn(x, n) for n in range(4)]
    return [choose([turned[(n - b) % 4] for n in range(4)], part) for b in range(4)]


def place_mask(phase, c):
    want = jnp.where((phase >> 2) == (c % 4), phase & 3, -1)
    return (lanes() >> 5) == want


def front_kernel(
    phases, valid, q_hbm, k_hbm, v_hbm, w_hbm, go_hbm,
    aq_hbm, ak_hbm, av_hbm, fq_hbm, own_hbm, q_far, do_far, d_far,
    q_s, k_s, v_s, w_s, go_s, g_s, e_s, ds_s, on_s, st_s, nd_s, at_s,
    kv_buf, q_own, do_own, fe_s, fq_s, fr_s, aq_s, ak_s, av_s,
    gw_s, a_send, a_recv, half_s, b_send, b_recv, c_buf, d_own,
    in_sem, out_sem, own_sem, kv_send, kv_recv, qd_send, qd_recv, pair_send, pair_recv,
    a_sem, b_ss, b_rs, c_ss, c_rs, d_ss, d_rs,
):
    dp, sq, tz = lax.axis_index("dp"), lax.axis_index("seq"), lax.axis_index("tensor")
    y, x, core = sq // 8, (sq % 8) // 2, sq % 2
    yx = sq // 2
    yg = dp * 2 + y

    copies = [
        pltpu.make_async_copy(k_hbm.at[0], k_s, in_sem.at[0]),
        pltpu.make_async_copy(v_hbm.at[0], v_s, in_sem.at[1]),
        pltpu.make_async_copy(q_hbm.at[0], q_s, in_sem.at[2]),
        pltpu.make_async_copy(w_hbm, w_s, in_sem.at[3]),
        pltpu.make_async_copy(go_hbm.at[0], go_s, in_sem.at[4]),
    ]
    for c in copies:
        c.start()

    def at_yx(k):
        yy, xx = (y + k // 4) % 2, (x + k % 4) % 4
        return yy * 4 + xx

    def from_yx(k):
        yy, xx = (y + 2 - k // 4) % 2, (x + 4 - k % 4) % 4
        return yy * 4 + xx

    same_core = [(dp, at_yx(k) * 2 + core, tz) for k in range(1, 8)]
    sibling = (dp, yx * 2 + 1 - core, tz)
    other_core = [(dp, (y * 4 + (x + k) % 4) * 2 + 1 - core, tz) for k in range(1, 4)]
    y_peers = []
    for k in range(1, 4):
        there = (yg + k) % 4
        y_peers.append((there // 2, (there % 2) * 8 + x * 2 + core, tz))
    barrier = pltpu.get_barrier_semaphore()
    dp_peers = [(1 - dp, yy * 8 + x * 2 + core, tz) for yy in range(2)]
    greet = same_core + [sibling] + other_core + dp_peers
    for peer in greet:
        pl.semaphore_signal(barrier, inc=1, device_id=peer, device_id_type=MESH)

    for c in copies[:2]:
        c.wait()
    for h in range(HEADS):
        ph = phases[h]
        kv_buf[core, h, yx, 0:DH, :] = pick(lambda o: k_s[h, :, pl.ds(o, 128)], ph).astype(BF16)
        kv_buf[core, h, yx, DH:2 * DH, :] = pick(lambda o: v_s[h, :, pl.ds(o, 128)], ph).astype(BF16)
    pl.semaphore_wait(barrier, len(greet))

    def gather(mine, slot, ss, rs, base):
        sends, recvs = [], []
        for k in range(1, 8):
            n = base + k - 1
            sends.append(pltpu.make_async_remote_copy(
                mine, slot(yx), ss.at[n], rs.at[n], device_id=same_core[k - 1], device_id_type=MESH))
            recvs.append(pltpu.make_async_remote_copy(
                mine, slot(from_yx(k)), ss.at[n], rs.at[n], device_id=same_core[k - 1], device_id_type=MESH))
        return sends, recvs

    def to_pair(buf, i):
        out = pltpu.make_async_remote_copy(
            buf(core), buf(core), pair_send.at[i], pair_recv.at[i], device_id=sibling, device_id_type=MESH)
        back = pltpu.make_async_remote_copy(
            buf(1 - core), buf(1 - core), pair_send.at[i], pair_recv.at[i], device_id=sibling, device_id_type=MESH)
        return out, back

    kv_out, kv_in, kv_pair = [], [], []
    for h in range(HEADS):
        sends, recvs = gather(kv_buf.at[core, h, yx], lambda n, h=h: kv_buf.at[core, h, n], kv_send, kv_recv, 7 * h)
        kv_out.append(sends)
        kv_in.append(recvs)
        kv_pair.append(to_pair(lambda c, h=h: kv_buf.at[c, h], h))
        for c in sends:
            c.start()

    copies[2].wait()
    for h in range(HEADS):
        q_own[h] = pick(lambda o: q_s[h, :, pl.ds(o, 128)], phases[h]).astype(BF16)
    own_copies = [
        pltpu.make_async_copy(kv_buf.at[core, h, yx], own_hbm.at[h], own_sem.at[h]) for h in range(HEADS)]
    own_copies.append(pltpu.make_async_copy(q_own, q_far.at[core, yx], own_sem.at[3]))
    for c in own_copies:
        c.start()

    def forward_pair(h):
        for c in kv_in[h]:
            c.wait_recv()
        kv_pair[h][0].start()

    def near_forward(u, carry):
        h, off = u // 2, pl.multiple_of((u % 2) * SEG, SEG)
        rows = pl.ds(off, SEG)
        k_t, v_t = k_s[h, :, rows], v_s[h, :, rows]
        qh, ql = hi_lo(q_s[h, :, rows].astype(F32) * (SCALE * LOG2E))
        kk = jnp.concatenate([k_t, k_t], 0).T
        s = nn(kk, jnp.concatenate([qh, ql], 0))
        m = jnp.max(s, axis=0, keepdims=True)
        e = jnp.exp2(s - m).astype(BF16)
        e_s[u] = e
        o = nn(jnp.concatenate([v_t, jnp.ones((16, SEG), BF16)], 0), e)
        total = o[DH:DH + 1]
        r = 1.0 / total
        on_s[h, :, rows] = o[:DH] * r
        st_s[h, 0:1, rows] = r
        st_s[h, 1:2, rows] = m + jnp.log2(total)
        return carry

    for u in range(2 * HEADS):
        near_forward(u, 0)
        if u == 3:
            forward_pair(0)
    forward_pair(1)
    copies[3].wait()
    copies[4].wait()
    g_s[...] = nt(w_s[...], go_s[...]).astype(BF16).reshape(HEADS, DH, ROWS)
    forward_pair(2)
    q_out, q_in = gather(q_own, lambda n: q_far.at[core, n], qd_send, qd_recv, 0)
    q_pair = to_pair(lambda c: q_far.at[c], HEADS)
    for c in q_out:
        c.start()

    key_index = lanes(SPAN)

    def all_cols(buf, h, lo, hi):
        return jnp.concatenate([buf[n % 2, h, n // 2, lo:hi, :] for n in range(PEERS)], 1)

    def far_forward(h, carry):
        ph = phases[h]
        k_t, v_t = all_cols(kv_buf, h, 0, DH), all_cols(kv_buf, h, DH, 2 * DH)
        q_t = q_own[h].astype(F32) * (SCALE * LOG2E)
        hi = q_t.astype(BF16).astype(F32)
        lhs = jnp.concatenate([hi, q_t - hi], 0).T.astype(BF16)
        s = nn(lhs, jnp.concatenate([k_t, k_t], 0))
        row = (key_index >> 5) * (RATE * BLK) + ph * BLK + (key_index & 31)
        s = jnp.where(row < valid[0], s, -1e30)
        m = jnp.max(s, axis=1, keepdims=True)
        e = jnp.exp2(s - m).astype(BF16)
        fe_s[h] = e
        o = nt(e, jnp.concatenate([v_t, jnp.ones((16, SPAN), BF16)], 0))
        total = o[:, DH:DH + 1]
        r = 1.0 / total
        packed = jnp.concatenate(
            [o[:, :DH] * r, jnp.broadcast_to(m + jnp.log2(total), (SUB, 32)), jnp.broadcast_to(r, (SUB, 32))], 1).T
        far_out, far_lse, far_r = packed[0:DH], packed[DH:DH + 1], packed[96:97]
        near_out = pick(lambda o: on_s[h, :, pl.ds(o, 128)], ph)
        near_lse = pick(lambda o: st_s[h, :, pl.ds(o, 128)], ph)[1:2]
        g = pick(lambda o: g_s[h, :, pl.ds(o, 128)], ph)
        mixing = 1.0 / (1.0 + jnp.exp2(near_lse - far_lse))
        rest = 1.0 / (1.0 + jnp.exp2(far_lse - near_lse))
        diff = far_out - near_out
        comb = near_out + mixing * diff
        far_dlse = jnp.sum(g * diff, axis=0, keepdims=True) * mixing * rest
        far_dout = (mixing * g).astype(BF16)
        fd = far_dout.astype(F32)
        term = far_dlse - jnp.sum(fd * far_out, axis=0, keepdims=True)
        do_own[h, 0:DH, :] = far_dout
        do_own[h, DH:DO_ROWS, :] = jnp.concatenate(
            [*split3(-far_lse), *split3(term), jnp.zeros((10, SUB), BF16)], 0)
        scaled = (fd * far_r).astype(BF16).astype(F32)
        term_r = far_dlse * far_r - jnp.sum(scaled * far_out, axis=0, keepdims=True)
        fr_s[h, 0:DH, :] = scaled
        fr_s[h, DH:DH + 8, :] = jnp.broadcast_to(term_r, (8, SUB))
        stack = jnp.concatenate([comb, rest, -far_dlse, jnp.zeros((6, SUB), F32)], 0)
        parts = place_parts(stack, ph)
        for c in range(16):
            cols = pl.ds(c * 128, 128)
            mask = place_mask(ph, c)
            part = parts[c // 4]
            near = on_s[h, :, cols]
            at_s[h, :, cols] = jnp.where(mask, part[:DH], near).astype(BF16)
            factor = jnp.where(mask, part[DH:DH + 1], 1.0)
            dlse = jnp.where(mask, part[DH + 1:DH + 2], 0.0)
            rr = st_s[h, 0:1, cols]
            nd = (g_s[h, :, cols].astype(F32) * factor).astype(BF16).astype(F32)
            nd = (nd * rr).astype(BF16)
            nd_s[h, :, cols] = nd
            st_s[h, 2:3, cols] = dlse * rr - jnp.sum(nd.astype(F32) * near, axis=0, keepdims=True)
        return carry

    for h in range(HEADS):
        kv_pair[h][1].wait_recv()
    for h in range(HEADS):
        far_forward(h, 0)

    do_out, do_in = gather(do_own, lambda n: do_far.at[core, n], qd_send, qd_recv, 7)
    do_pair = to_pair(lambda c: do_far.at[c], HEADS + 1)
    for c in do_out:
        c.start()
    do_copy = pltpu.make_async_copy(do_own, do_far.at[core, yx], own_sem.at[4])
    do_copy.start()

    gw_s[...] = nn(at_s[...].reshape(HEADS * DH, ROWS), go_s[...])
    half = HEADS * DH // 2
    a_send[...] = gw_s[pl.ds(pl.multiple_of((1 - core) * half, 32), half), :].astype(BF16)
    a_copy = pltpu.make_async_remote_copy(a_send, a_recv, a_sem.at[0], a_sem.at[1], device_id=sibling, device_id_type=MESH)
    a_copy.start()

    def far_backward_q(h, carry):
        k_t, v_t = all_cols(kv_buf, h, 0, DH), all_cols(kv_buf, h, DH, 2 * DH)
        d = fr_s[h]
        term = d[DH:DH + 1]
        term_hi = term.astype(BF16).astype(F32)
        left = jnp.concatenate([d[:DH], term_hi, term - term_hi, jnp.zeros((62, SUB), F32)], 0).T.astype(BF16)
        ones = jnp.concatenate([jnp.ones((2, SPAN), BF16), jnp.zeros((62, SPAN), BF16)], 0)
        dprob = nn(left, jnp.concatenate([v_t, ones], 0))
        dscore = dprob.astype(BF16) * fe_s[h]
        fq_s[h] = nt(dscore, k_t).T * SCALE
        return carry

    for h in range(HEADS):
        far_backward_q(h, 0)
    fq_copy = pltpu.make_async_copy(fq_s, fq_hbm, own_sem.at[5])
    fq_copy.start()

    quarter, wide = half // 2, D // 2
    b_out, b_in = [], []
    for k in range(1, 4):
        b_out.append(pltpu.make_async_remote_copy(
            b_send.at[(x + k) % 4], b_recv.at[x], b_ss.at[k - 1], b_rs.at[k - 1],
            device_id=same_core[k - 1], device_id_type=MESH))
        b_in.append(pltpu.make_async_remote_copy(
            b_send.at[(x + k) % 4], b_recv.at[(x + 4 - k) % 4], b_ss.at[k - 1], b_rs.at[k - 1],
            device_id=same_core[k - 1], device_id_type=MESH))
    c_out, c_in = [], []
    for k in range(1, 4):
        c_out.append(pltpu.make_async_remote_copy(
            c_buf.at[yg], c_buf.at[yg], c_ss.at[k - 1], c_rs.at[k - 1], device_id=y_peers[k - 1], device_id_type=MESH))
        there = (yg + 4 - k) % 4
        c_in.append(pltpu.make_async_remote_copy(
            c_buf.at[there], c_buf.at[there], c_ss.at[k - 1], c_rs.at[k - 1], device_id=y_peers[k - 1], device_id_type=MESH))
    d_out, d_in = [], []
    d_peers = [same_core[k - 1] for k in range(1, 4)] + [sibling] + other_core
    for k in range(1, 8):
        d_out.append(pltpu.make_async_remote_copy(
            d_own, d_far.at[core, x], d_ss.at[k - 1], d_rs.at[k - 1], device_id=d_peers[k - 1], device_id_type=MESH))
        theirs = d_far.at[core if k < 4 else 1 - core, (x + 4 - k % 4) % 4]
        d_in.append(pltpu.make_async_remote_copy(
            d_own, theirs, d_ss.at[k - 1], d_rs.at[k - 1], device_id=d_peers[k - 1], device_id_type=MESH))
    d_copy = pltpu.make_async_copy(d_own, d_far.at[core, x], own_sem.at[6])

    def outs(h):
        return [
            pltpu.make_async_copy(aq_s.at[h], aq_hbm.at[h], out_sem.at[0, h]),
            pltpu.make_async_copy(ak_s.at[h], ak_hbm.at[h], out_sem.at[1, h]),
            pltpu.make_async_copy(av_s.at[h], av_hbm.at[h], out_sem.at[2, h]),
        ]


    def near_backward(u, carry):
        h, off = u // 2, pl.multiple_of((u % 2) * SEG, SEG)
        rows = pl.ds(off, SEG)
        q_t, k_t, v_t, gh = q_s[h, :, rows], k_s[h, :, rows], v_s[h, :, rows], nd_s[h, :, rows]
        th, tl = hi_lo(st_s[h, 2:3, rows])
        gg = jnp.concatenate([gh, jnp.concatenate([th, tl, jnp.zeros((14, SEG), BF16)], 0)], 0)
        vv = jnp.concatenate([v_t, jnp.ones((2, SEG), BF16), jnp.zeros((14, SEG), BF16)], 0).T
        for ib in range(2):
            cols = slice(ib * 512, ib * 512 + 512)
            dprob = nn(vv, gg[:, cols])
            ds = dprob.astype(BF16) * e_s[u, :, cols]
            ds_s[:, cols] = ds
            aq_s[h, :, pl.ds(pl.multiple_of(off + ib * 512, 512), 512)] = (nn(k_t, ds) * SCALE).astype(BF16)
        for jb in range(2):
            cols = slice(jb * 512, jb * 512 + 512)
            out_cols = pl.ds(pl.multiple_of(off + jb * 512, 512), 512)
            ak_s[h, :, out_cols] = (nt(ds_s[cols, :], q_t).T * SCALE).astype(BF16)
            av_s[h, :, out_cols] = nt(e_s[u, cols, :], gh).T.astype(BF16)

        @pl.when(u % 2 == 1)
        def _():
            for c in outs(h):
                c.start()

        @pl.when(u == 0)
        def _():
            for c in own_copies:
                c.wait()
            for c in q_in:
                c.wait_recv()
            q_pair[0].start()
            a_copy.wait()
            mine = gw_s[pl.ds(pl.multiple_of(core * half, 32), half), :]
            half_s[...] = mine + a_recv[...].astype(F32)
            for t in range(4):
                b_send[t] = half_s[(t // 2) * quarter:(t // 2 + 1) * quarter, (t % 2) * wide:(t % 2 + 1) * wide].astype(BF16)
            for c in b_out:
                c.start()

        @pl.when(u == 3)
        def _():
            for c in b_in:
                c.wait_recv()
            b_recv[x] = b_send[x]
            total = b_recv[0].astype(F32)
            for t in range(1, 4):
                total = total + b_recv[t].astype(F32)
            c_buf[yg] = total.astype(BF16)
            for c in c_out:
                c.start()

        @pl.when(u == 4)
        def _():
            for c in do_in:
                c.wait_recv()
            do_copy.wait()
            do_pair[0].start()
            for c in c_in:
                c.wait_recv()
            total = c_buf[0].astype(F32)
            for t in range(1, 4):
                total = total + c_buf[t].astype(F32)
            d_own[...] = total.astype(BF16)
            for c in d_out:
                c.start()
            d_copy.start()

        return carry

    lax.fori_loop(0, 2 * HEADS, near_backward, 0)
    fq_copy.wait()
    d_copy.wait()
    for sends in kv_out:
        for c in sends:
            c.wait_send()
    for pair in kv_pair + [q_pair, do_pair]:
        pair[0].wait_send()
    for c in q_out + do_out + b_out + c_out + d_out:
        c.wait_send()
    q_pair[1].wait_recv()
    do_pair[1].wait_recv()
    for c in d_in:
        c.wait_recv()
    for h in range(HEADS):
        for c in outs(h):
            c.wait()


def back_kernel(
    phases, valid, aq_hbm, ak_hbm, av_hbm, fq_hbm, own_hbm, q_far, do_far, d_far,
    dq_hbm, dk_hbm, dv_hbm, gw_hbm,
    aq_s, ak_s, av_s, fq_s, own_s, q_buf, do_buf, d_buf, oq_s, ok_s, ov_s, gw_s, in_sem, out_sem,
):
    sq = lax.axis_index("seq")
    pairs = ((q_far, q_buf), (own_hbm, own_s), (do_far, do_buf), (fq_hbm, fq_s),
             (aq_hbm, aq_s), (ak_hbm, ak_s), (av_hbm, av_s), (d_far, d_buf))
    copies = [pltpu.make_async_copy(a, b, in_sem.at[n]) for n, (a, b) in enumerate(pairs)]
    for c in copies:
        c.start()

    def all_cols(buf, h, lo, hi):
        return jnp.concatenate([buf[n % 2, n // 2, h, lo:hi, :] for n in range(PEERS)], 1)

    def far_backward_kv(h):
        ph = phases[h]
        q_t, do_t = all_cols(q_buf, h, 0, DH), all_cols(do_buf, h, 0, DH)
        stats = all_cols(do_buf, h, DH, DO_ROWS)
        own_k = own_s[h, 0:DH, :].astype(F32) * (SCALE * LOG2E)
        own_v = own_s[h, DH:2 * DH, :].astype(F32)
        hi = own_k.astype(BF16).astype(F32)
        index = lax.broadcasted_iota(jnp.int32, (16, SUB), 0)
        first = jnp.where(index < 3, 1.0, 0.0)
        second = jnp.where((index >= 3) & (index < 6), 1.0, 0.0)
        zeros = jnp.zeros((48, SUB), F32)
        left_s = jnp.concatenate([hi, own_k - hi, first, zeros, zeros, jnp.zeros((16, SUB), F32)], 0).T.astype(BF16)
        s = nn(left_s[:, :QD_ROWS], jnp.concatenate([q_t, q_t, stats], 0))
        j = lax.broadcasted_iota(jnp.int32, (SUB, 1), 0)
        row = sq * ROWS + (j >> 5) * (RATE * BLK) + ph * BLK + (j & 31)
        probs = jnp.where(row < valid[0], jnp.exp2(s), 0.0).astype(BF16)
        left_d = jnp.concatenate([own_v, second, zeros], 0).T.astype(BF16)
        dprob = nn(left_d[:, :DH + 16], jnp.concatenate([do_t, stats], 0))
        dscore = dprob.astype(BF16) * probs
        return jnp.concatenate([nt(dscore, q_t) * SCALE, nt(probs, do_t)], 1).T

    for c in copies[:3]:
        c.wait()
    both = [far_backward_kv(h) for h in range(HEADS)]
    for c in copies[3:]:
        c.wait()
    outs = []
    for h in range(HEADS):
        ph = phases[h]
        parts_k, parts_v = place_parts(both[h][:DH], ph), place_parts(both[h][DH:], ph)
        parts_q = place_parts(fq_s[h], ph)
        for c in range(16):
            cols = pl.ds(c * 128, 128)
            mask = place_mask(ph, c)
            for out, near, parts in ((oq_s, aq_s, parts_q), (ok_s, ak_s, parts_k), (ov_s, av_s, parts_v)):
                out[h, :, cols] = (near[h, :, cols].astype(F32) + jnp.where(mask, parts[c // 4], 0.0)).astype(BF16)
        for n, (a, b) in enumerate(((oq_s, dq_hbm), (ok_s, dk_hbm), (ov_s, dv_hbm))):
            outs.append(pltpu.make_async_copy(a.at[h], b.at[0, h], out_sem.at[n, h]))
            outs[-1].start()
    half, quarter, wide = HEADS * DH // 2, HEADS * DH // 4, D // 2
    for cc in range(2):
        for t in range(4):
            gw_s[cc * half + (t // 2) * quarter:cc * half + (t // 2 + 1) * quarter, (t % 2) * wide:(t % 2 + 1) * wide] = (
                d_buf[cc, t].astype(F32))
    outs.append(pltpu.make_async_copy(gw_s, gw_hbm, out_sem.at[3, 0]))
    outs[-1].start()
    for c in outs:
        c.wait()


def shards(queries, key_states, value_states, out_weight, grad_output, phases, valid_rows):
    big = lambda dtype: pltpu.VMEM((HEADS, DH, ROWS), dtype)
    dma = pltpu.SemaphoreType.DMA
    any_spec = pl.BlockSpec(memory_space=pl.ANY)
    smem = pl.BlockSpec(memory_space=pltpu.SMEM)
    chunk = (HEADS * DH // 4, D // 2)
    state = jax.ShapeDtypeStruct(queries.shape, BF16)
    near = jax.ShapeDtypeStruct((HEADS, DH, ROWS), BF16)
    shape = jax.ShapeDtypeStruct
    passed = [
        near, near, near, shape((HEADS, DH, SUB), F32), shape((HEADS, 2 * DH, SUB), BF16),
        shape((2, 8, HEADS, DH, SUB), BF16), shape((2, 8, HEADS, DO_ROWS, SUB), BF16), shape((2, 4, *chunk), BF16)]
    between = pl.pallas_call(
        front_kernel,
        out_shape=passed,
        in_specs=[smem, smem] + [any_spec] * 5,
        out_specs=[any_spec] * 8,
        scratch_shapes=[
            big(BF16), big(BF16), big(BF16),
            pltpu.VMEM((HEADS * DH, D), BF16), pltpu.VMEM((ROWS, D), BF16),
            big(BF16),
            pltpu.VMEM((2 * HEADS, SEG, SEG), BF16), pltpu.VMEM((SEG, SEG), BF16),
            big(F32), pltpu.VMEM((HEADS, 8, ROWS), F32), big(BF16), big(BF16),
            pltpu.VMEM((2, HEADS, 8, 2 * DH, SUB), BF16),
            pltpu.VMEM((HEADS, DH, SUB), BF16), pltpu.VMEM((HEADS, DO_ROWS, SUB), BF16),
            pltpu.VMEM((HEADS, SUB, SPAN), BF16), pltpu.VMEM((HEADS, DH, SUB), F32), pltpu.VMEM((HEADS, DH + 8, SUB), F32),
            big(BF16), big(BF16), big(BF16),
            pltpu.VMEM((HEADS * DH, D), F32),
            pltpu.VMEM((HEADS * DH // 2, D), BF16), pltpu.VMEM((HEADS * DH // 2, D), BF16),
            pltpu.VMEM((HEADS * DH // 2, D), F32),
            pltpu.VMEM((4, *chunk), BF16), pltpu.VMEM((4, *chunk), BF16), pltpu.VMEM((4, *chunk), BF16),
            pltpu.VMEM(chunk, BF16),
            dma((5,)), dma((3, HEADS)), dma((7,)), dma((21,)), dma((21,)), dma((14,)), dma((14,)), dma((5,)), dma((5,)),
            dma((2,)), dma((3,)), dma((3,)), dma((3,)), dma((3,)), dma((7,)), dma((7,)),
        ],
        compiler_params=pltpu.CompilerParams(
            collective_id=0, has_side_effects=True, vmem_limit_bytes=58 << 20),
        name="front",
    )(phases, valid_rows, queries, key_states, value_states, out_weight, grad_output)
    return pl.pallas_call(
        back_kernel,
        out_shape=[state, state, state, shape((HEADS * DH, D), F32)],
        in_specs=[smem, smem] + [any_spec] * 8,
        out_specs=[any_spec] * 4,
        scratch_shapes=[pltpu.VMEM(p.shape, p.dtype) for p in passed] + [
            big(BF16), big(BF16), big(BF16), pltpu.VMEM((HEADS * DH, D), F32), dma((8,)), dma((4, HEADS))],
        compiler_params=pltpu.CompilerParams(vmem_limit_bytes=58 << 20),
        name="back",
    )(phases, valid_rows, *between)


def solution(mesh):
    heads = P("dp", "tensor", None, "seq")
    return jax.shard_map(
        shards, mesh=mesh,
        in_specs=(heads, heads, heads, P("tensor", None), P("dp", "seq", None), P("tensor"), P("dp")),
        out_specs=(heads, heads, heads, P("tensor", None)),
        check_vma=False,
    )
```

```python
import jax
import jax.numpy as jnp
from jax import lax
from jax.experimental import pallas as pl
from jax.experimental.pallas import tpu as pltpu
from jax.sharding import PartitionSpec as P

F32 = jnp.float32
BF16 = jnp.bfloat16
SEG = 1024
RATE = 16
BLK = 32
HEADS = 3
DH = 64
ROWS = 2048
SUB = ROWS // RATE
D = 768
PEERS = 16
SPAN = PEERS * SUB
SCALE = 0.125
LOG2E = 1.4426950408889634
DO_ROWS = 80
QD_ROWS = DH + DO_ROWS
MESH = pl.DeviceIdType.MESH


def nn(a, b):
    return jnp.dot(a, b, preferred_element_type=F32)


def nt(a, b):
    return lax.dot_general(a, b, (((1,), (1,)), ((), ())), preferred_element_type=F32)


def hi_lo(x):
    hi = x.astype(BF16)
    return hi, (x - hi.astype(F32)).astype(BF16)


def split3(x):
    hi = x.astype(BF16)
    rest = x - hi.astype(F32)
    mid = rest.astype(BF16)
    return hi, mid, (rest - mid.astype(F32)).astype(BF16)


def lanes(n=SUB):
    return lax.broadcasted_iota(jnp.int32, (1, n), 1)


def turn(x, groups):
    groups = groups % 4
    return x if groups == 0 else pltpu.roll(x, groups * 32, 1)


def choose(options, which):
    out = options[0]
    for n in range(1, len(options)):
        out = jnp.where(which == n, options[n], out)
    return out


def pick(load, phase):
    chunk = jnp.full((1, SUB), phase >> 2, jnp.int32)
    part = jnp.full((1, SUB), phase & 3, jnp.int32)
    group = lanes() >> 5
    out = None
    for b in range(4):
        x = choose([load(b * 512 + n * 128).astype(F32) for n in range(4)], chunk)
        x = choose([turn(x, b - n) for n in range(4)], part)
        out = x if b == 0 else jnp.where(group == b, x, out)
    return out


def place_parts(x, phase):
    part = jnp.full((1, SUB), phase & 3, jnp.int32)
    turned = [turn(x, n) for n in range(4)]
    return [choose([turned[(n - b) % 4] for n in range(4)], part) for b in range(4)]


def place_mask(phase, c):
    want = jnp.where((phase >> 2) == (c % 4), phase & 3, -1)
    return (lanes() >> 5) == want


def front_kernel(
    phases, valid, q_hbm, k_hbm, v_hbm, w_hbm, go_hbm,
    aq_hbm, ak_hbm, av_hbm, fq_hbm, own_hbm, q_far, do_far, d_far,
    q_s, k_s, v_s, w_s, go_s, g_s, e_s, ds_s, on_s, st_s, nd_s, at_s,
    kv_buf, q_own, do_own, fe_s, fq_s, fr_s, aq_s, ak_s, av_s,
    gw_s, a_send, a_recv, half_s, b_send, b_recv, c_buf, d_own,
    in_sem, out_sem, own_sem, kv_send, kv_recv, qd_send, qd_recv, pair_send, pair_recv,
    a_sem, b_ss, b_rs, c_ss, c_rs, d_ss, d_rs,
):
    dp, sq, tz = lax.axis_index("dp"), lax.axis_index("seq"), lax.axis_index("tensor")
    y, x, core = sq // 8, (sq % 8) // 2, sq % 2
    yx = sq // 2
    yg = dp * 2 + y

    copies = [
        pltpu.make_async_copy(k_hbm.at[0], k_s, in_sem.at[0]),
        pltpu.make_async_copy(v_hbm.at[0], v_s, in_sem.at[1]),
        pltpu.make_async_copy(q_hbm.at[0], q_s, in_sem.at[2]),
        pltpu.make_async_copy(w_hbm, w_s, in_sem.at[3]),
        pltpu.make_async_copy(go_hbm.at[0], go_s, in_sem.at[4]),
    ]
    for c in copies:
        c.start()

    def at_yx(k):
        yy, xx = (y + k // 4) % 2, (x + k % 4) % 4
        return yy * 4 + xx

    def from_yx(k):
        yy, xx = (y + 2 - k // 4) % 2, (x + 4 - k % 4) % 4
        return yy * 4 + xx

    same_core = [(dp, at_yx(k) * 2 + core, tz) for k in range(1, 8)]
    sibling = (dp, yx * 2 + 1 - core, tz)
    other_core = [(dp, (y * 4 + (x + k) % 4) * 2 + 1 - core, tz) for k in range(1, 4)]
    y_peers = []
    for k in range(1, 4):
        there = (yg + k) % 4
        y_peers.append((there // 2, (there % 2) * 8 + x * 2 + core, tz))
    barrier = pltpu.get_barrier_semaphore()
    dp_peers = [(1 - dp, yy * 8 + x * 2 + core, tz) for yy in range(2)]
    greet = same_core + [sibling] + other_core + dp_peers
    for peer in greet:
        pl.semaphore_signal(barrier, inc=1, device_id=peer, device_id_type=MESH)

    for c in copies[:2]:
        c.wait()
    for h in range(HEADS):
        ph = phases[h]
        kv_buf[core, h, yx, 0:DH, :] = pick(lambda o: k_s[h, :, pl.ds(o, 128)], ph).astype(BF16)
        kv_buf[core, h, yx, DH:2 * DH, :] = pick(lambda o: v_s[h, :, pl.ds(o, 128)], ph).astype(BF16)
    pl.semaphore_wait(barrier, len(greet))

    def gather(mine, slot, ss, rs, base):
        sends, recvs = [], []
        for k in range(1, 8):
            n = base + k - 1
            sends.append(pltpu.make_async_remote_copy(
                mine, slot(yx), ss.at[n], rs.at[n], device_id=same_core[k - 1], device_id_type=MESH))
            recvs.append(pltpu.make_async_remote_copy(
                mine, slot(from_yx(k)), ss.at[n], rs.at[n], device_id=same_core[k - 1], device_id_type=MESH))
        return sends, recvs

    def to_pair(buf, i):
        out = pltpu.make_async_remote_copy(
            buf(core), buf(core), pair_send.at[i], pair_recv.at[i], device_id=sibling, device_id_type=MESH)
        back = pltpu.make_async_remote_copy(
            buf(1 - core), buf(1 - core), pair_send.at[i], pair_recv.at[i], device_id=sibling, device_id_type=MESH)
        return out, back

    kv_out, kv_in, kv_pair = [], [], []
    for h in range(HEADS):
        sends, recvs = gather(kv_buf.at[core, h, yx], lambda n, h=h: kv_buf.at[core, h, n], kv_send, kv_recv, 7 * h)
        kv_out.append(sends)
        kv_in.append(recvs)
        kv_pair.append(to_pair(lambda c, h=h: kv_buf.at[c, h], h))
        for c in sends:
            c.start()

    copies[2].wait()
    for h in range(HEADS):
        q_own[h] = pick(lambda o: q_s[h, :, pl.ds(o, 128)], phases[h]).astype(BF16)
    own_copies = [
        pltpu.make_async_copy(kv_buf.at[core, h, yx], own_hbm.at[h], own_sem.at[h]) for h in range(HEADS)]
    own_copies.append(pltpu.make_async_copy(q_own, q_far.at[core, yx], own_sem.at[3]))
    for c in own_copies:
        c.start()

    def forward_pair(h):
        for c in kv_in[h]:
            c.wait_recv()
        kv_pair[h][0].start()

    def near_forward(u, carry):
        h, off = u // 2, pl.multiple_of((u % 2) * SEG, SEG)
        rows = pl.ds(off, SEG)
        k_t, v_t = k_s[h, :, rows], v_s[h, :, rows]
        qh, ql = hi_lo(q_s[h, :, rows].astype(F32) * (SCALE * LOG2E))
        kk = jnp.concatenate([k_t, k_t], 0).T
        s = nn(kk, jnp.concatenate([qh, ql], 0))
        m = jnp.max(s, axis=0, keepdims=True)
        e = jnp.exp2(s - m).astype(BF16)
        e_s[u] = e
        o = nn(jnp.concatenate([v_t, jnp.ones((16, SEG), BF16)], 0), e)
        total = o[DH:DH + 1]
        r = 1.0 / total
        on_s[h, :, rows] = o[:DH] * r
        st_s[h, 0:1, rows] = r
        st_s[h, 1:2, rows] = m + jnp.log2(total)
        return carry

    for u in range(2 * HEADS):
        near_forward(u, 0)
        if u == 3:
            forward_pair(0)
    forward_pair(1)
    copies[3].wait()
    copies[4].wait()
    g_s[...] = nt(w_s[...], go_s[...]).astype(BF16).reshape(HEADS, DH, ROWS)
    forward_pair(2)
    q_out, q_in = gather(q_own, lambda n: q_far.at[core, n], qd_send, qd_recv, 0)
    q_pair = to_pair(lambda c: q_far.at[c], HEADS)
    for c in q_out:
        c.start()

    key_index = lanes(SPAN)

    def all_cols(buf, h, lo, hi):
        return jnp.concatenate([buf[n % 2, h, n // 2, lo:hi, :] for n in range(PEERS)], 1)

    def far_forward(h, carry):
        ph = phases[h]
        k_t, v_t = all_cols(kv_buf, h, 0, DH), all_cols(kv_buf, h, DH, 2 * DH)
        q_t = q_own[h].astype(F32) * (SCALE * LOG2E)
        hi = q_t.astype(BF16).astype(F32)
        lhs = jnp.concatenate([hi, q_t - hi], 0).T.astype(BF16)
        s = nn(lhs, jnp.concatenate([k_t, k_t], 0))
        row = (key_index >> 5) * (RATE * BLK) + ph * BLK + (key_index & 31)
        s = jnp.where(row < valid[0], s, -1e30)
        m = jnp.max(s, axis=1, keepdims=True)
        e = jnp.exp2(s - m).astype(BF16)
        fe_s[h] = e
        o = nt(e, jnp.concatenate([v_t, jnp.ones((16, SPAN), BF16)], 0))
        total = o[:, DH:DH + 1]
        r = 1.0 / total
        packed = jnp.concatenate(
            [o[:, :DH] * r, jnp.broadcast_to(m + jnp.log2(total), (SUB, 32)), jnp.broadcast_to(r, (SUB, 32))], 1).T
        far_out, far_lse, far_r = packed[0:DH], packed[DH:DH + 1], packed[96:97]
        near_out = pick(lambda o: on_s[h, :, pl.ds(o, 128)], ph)
        near_lse = pick(lambda o: st_s[h, :, pl.ds(o, 128)], ph)[1:2]
        g = pick(lambda o: g_s[h, :, pl.ds(o, 128)], ph)
        mixing = 1.0 / (1.0 + jnp.exp2(near_lse - far_lse))
        rest = 1.0 / (1.0 + jnp.exp2(far_lse - near_lse))
        diff = far_out - near_out
        comb = near_out + mixing * diff
        far_dlse = jnp.sum(g * diff, axis=0, keepdims=True) * mixing * rest
        far_dout = (mixing * g).astype(BF16)
        fd = far_dout.astype(F32)
        term = far_dlse - jnp.sum(fd * far_out, axis=0, keepdims=True)
        do_own[h, 0:DH, :] = far_dout
        do_own[h, DH:DO_ROWS, :] = jnp.concatenate(
            [*split3(-far_lse), *split3(term), jnp.zeros((10, SUB), BF16)], 0)
        scaled = (fd * far_r).astype(BF16).astype(F32)
        term_r = far_dlse * far_r - jnp.sum(scaled * far_out, axis=0, keepdims=True)
        fr_s[h, 0:DH, :] = scaled
        fr_s[h, DH:DH + 8, :] = jnp.broadcast_to(term_r, (8, SUB))
        stack = jnp.concatenate([comb, rest, -far_dlse, jnp.zeros((6, SUB), F32)], 0)
        parts = place_parts(stack, ph)
        for c in range(16):
            cols = pl.ds(c * 128, 128)
            mask = place_mask(ph, c)
            part = parts[c // 4]
            near = on_s[h, :, cols]
            at_s[h, :, cols] = jnp.where(mask, part[:DH], near).astype(BF16)
            factor = jnp.where(mask, part[DH:DH + 1], 1.0)
            dlse = jnp.where(mask, part[DH + 1:DH + 2], 0.0)
            rr = st_s[h, 0:1, cols]
            nd = (g_s[h, :, cols].astype(F32) * factor).astype(BF16).astype(F32)
            nd = (nd * rr).astype(BF16)
            nd_s[h, :, cols] = nd
            st_s[h, 2:3, cols] = dlse * rr - jnp.sum(nd.astype(F32) * near, axis=0, keepdims=True)
        return carry

    for h in range(HEADS):
        kv_pair[h][1].wait_recv()
    for h in range(HEADS):
        far_forward(h, 0)

    do_out, do_in = [], []
    for h in range(HEADS):
        sends, recvs = gather(do_own.at[h], lambda n, h=h: do_far.at[core, n, h], qd_send, qd_recv, 7 + 7 * h)
        do_out += sends
        do_in += recvs
    do_pair = to_pair(lambda c: do_far.at[c], HEADS + 1)
    for c in do_out[:14]:
        c.start()
    do_copy = pltpu.make_async_copy(do_own, do_far.at[core, yx], own_sem.at[4])
    do_copy.start()

    gw_s[...] = nn(at_s[...].reshape(HEADS * DH, ROWS), go_s[...])
    half = HEADS * DH // 2
    a_send[...] = gw_s[pl.ds(pl.multiple_of((1 - core) * half, 32), half), :].astype(BF16)
    a_copy = pltpu.make_async_remote_copy(a_send, a_recv, a_sem.at[0], a_sem.at[1], device_id=sibling, device_id_type=MESH)
    a_copy.start()

    def far_backward_q(h, carry):
        k_t, v_t = all_cols(kv_buf, h, 0, DH), all_cols(kv_buf, h, DH, 2 * DH)
        d = fr_s[h]
        term = d[DH:DH + 1]
        term_hi = term.astype(BF16).astype(F32)
        left = jnp.concatenate([d[:DH], term_hi, term - term_hi, jnp.zeros((62, SUB), F32)], 0).T.astype(BF16)
        ones = jnp.concatenate([jnp.ones((2, SPAN), BF16), jnp.zeros((62, SPAN), BF16)], 0)
        dprob = nn(left, jnp.concatenate([v_t, ones], 0))
        dscore = dprob.astype(BF16) * fe_s[h]
        fq_s[h] = nt(dscore, k_t).T * SCALE
        return carry

    for h in range(HEADS):
        far_backward_q(h, 0)
    fq_copy = pltpu.make_async_copy(fq_s, fq_hbm, own_sem.at[5])
    fq_copy.start()

    quarter, wide = half // 2, D // 2
    b_out, b_in = [], []
    for k in range(1, 4):
        b_out.append(pltpu.make_async_remote_copy(
            b_send.at[(x + k) % 4], b_recv.at[x], b_ss.at[k - 1], b_rs.at[k - 1],
            device_id=same_core[k - 1], device_id_type=MESH))
        b_in.append(pltpu.make_async_remote_copy(
            b_send.at[(x + k) % 4], b_recv.at[(x + 4 - k) % 4], b_ss.at[k - 1], b_rs.at[k - 1],
            device_id=same_core[k - 1], device_id_type=MESH))
    c_out, c_in = [], []
    for k in range(1, 4):
        c_out.append(pltpu.make_async_remote_copy(
            c_buf.at[yg], c_buf.at[yg], c_ss.at[k - 1], c_rs.at[k - 1], device_id=y_peers[k - 1], device_id_type=MESH))
        there = (yg + 4 - k) % 4
        c_in.append(pltpu.make_async_remote_copy(
            c_buf.at[there], c_buf.at[there], c_ss.at[k - 1], c_rs.at[k - 1], device_id=y_peers[k - 1], device_id_type=MESH))
    d_out, d_in = [], []
    d_peers = [same_core[k - 1] for k in range(1, 4)] + [sibling] + other_core
    for k in range(1, 8):
        d_out.append(pltpu.make_async_remote_copy(
            d_own, d_far.at[core, x], d_ss.at[k - 1], d_rs.at[k - 1], device_id=d_peers[k - 1], device_id_type=MESH))
        theirs = d_far.at[core if k < 4 else 1 - core, (x + 4 - k % 4) % 4]
        d_in.append(pltpu.make_async_remote_copy(
            d_own, theirs, d_ss.at[k - 1], d_rs.at[k - 1], device_id=d_peers[k - 1], device_id_type=MESH))
    d_copy = pltpu.make_async_copy(d_own, d_far.at[core, x], own_sem.at[6])

    def outs(h):
        return [
            pltpu.make_async_copy(aq_s.at[h], aq_hbm.at[h], out_sem.at[0, h]),
            pltpu.make_async_copy(ak_s.at[h], ak_hbm.at[h], out_sem.at[1, h]),
            pltpu.make_async_copy(av_s.at[h], av_hbm.at[h], out_sem.at[2, h]),
        ]


    def near_backward(u, carry):
        h, off = u // 2, pl.multiple_of((u % 2) * SEG, SEG)
        rows = pl.ds(off, SEG)
        q_t, k_t, v_t, gh = q_s[h, :, rows], k_s[h, :, rows], v_s[h, :, rows], nd_s[h, :, rows]
        th, tl = hi_lo(st_s[h, 2:3, rows])
        gg = jnp.concatenate([gh, jnp.concatenate([th, tl, jnp.zeros((14, SEG), BF16)], 0)], 0)
        vv = jnp.concatenate([v_t, jnp.ones((2, SEG), BF16), jnp.zeros((14, SEG), BF16)], 0).T
        for ib in range(2):
            cols = slice(ib * 512, ib * 512 + 512)
            dprob = nn(vv, gg[:, cols])
            ds = dprob.astype(BF16) * e_s[u, :, cols]
            ds_s[:, cols] = ds
            aq_s[h, :, pl.ds(pl.multiple_of(off + ib * 512, 512), 512)] = (nn(k_t, ds) * SCALE).astype(BF16)
        for jb in range(2):
            cols = slice(jb * 512, jb * 512 + 512)
            out_cols = pl.ds(pl.multiple_of(off + jb * 512, 512), 512)
            ak_s[h, :, out_cols] = (nt(ds_s[cols, :], q_t).T * SCALE).astype(BF16)
            av_s[h, :, out_cols] = nt(e_s[u, cols, :], gh).T.astype(BF16)

        @pl.when(u % 2 == 1)
        def _():
            for c in outs(h):
                c.start()

        @pl.when(u == 0)
        def _():
            for c in own_copies:
                c.wait()
            for c in q_in:
                c.wait_recv()
            q_pair[0].start()
            a_copy.wait()
            mine = gw_s[pl.ds(pl.multiple_of(core * half, 32), half), :]
            half_s[...] = mine + a_recv[...].astype(F32)
            for t in range(4):
                b_send[t] = half_s[(t // 2) * quarter:(t // 2 + 1) * quarter, (t % 2) * wide:(t % 2 + 1) * wide].astype(BF16)
            for c in b_out + do_out[14:]:
                c.start()

        @pl.when(u == 1)
        def _():
            for c in b_in:
                c.wait_recv()
            b_recv[x] = b_send[x]
            total = b_recv[0].astype(F32)
            for t in range(1, 4):
                total = total + b_recv[t].astype(F32)
            c_buf[yg] = total.astype(BF16)
            for c in c_out:
                c.start()

        @pl.when(u == 3)
        def _():
            for c in c_in:
                c.wait_recv()
            total = c_buf[0].astype(F32)
            for t in range(1, 4):
                total = total + c_buf[t].astype(F32)
            d_own[...] = total.astype(BF16)
            for c in d_out:
                c.start()
            d_copy.start()

        @pl.when(u == 4)
        def _():
            for c in do_in:
                c.wait_recv()
            do_copy.wait()
            do_pair[0].start()

        return carry

    lax.fori_loop(0, 2 * HEADS, near_backward, 0)
    fq_copy.wait()
    d_copy.wait()
    for sends in kv_out:
        for c in sends:
            c.wait_send()
    for pair in kv_pair + [q_pair, do_pair]:
        pair[0].wait_send()
    for c in q_out + do_out + b_out + c_out + d_out:
        c.wait_send()
    q_pair[1].wait_recv()
    do_pair[1].wait_recv()
    for c in d_in:
        c.wait_recv()
    for h in range(HEADS):
        for c in outs(h):
            c.wait()


def back_kernel(
    phases, valid, aq_hbm, ak_hbm, av_hbm, fq_hbm, own_hbm, q_far, do_far, d_far,
    dq_hbm, dk_hbm, dv_hbm, gw_hbm,
    aq_s, ak_s, av_s, fq_s, own_s, q_buf, do_buf, d_buf, oq_s, ok_s, ov_s, gw_s, in_sem, out_sem,
):
    sq = lax.axis_index("seq")
    pairs = ((q_far, q_buf), (own_hbm, own_s), (do_far, do_buf), (fq_hbm, fq_s),
             (aq_hbm, aq_s), (ak_hbm, ak_s), (av_hbm, av_s), (d_far, d_buf))
    copies = [pltpu.make_async_copy(a, b, in_sem.at[n]) for n, (a, b) in enumerate(pairs)]
    for c in copies:
        c.start()

    def all_cols(buf, h, lo, hi):
        return jnp.concatenate([buf[n % 2, n // 2, h, lo:hi, :] for n in range(PEERS)], 1)

    def far_backward_kv(h):
        ph = phases[h]
        q_t, do_t = all_cols(q_buf, h, 0, DH), all_cols(do_buf, h, 0, DH)
        stats = all_cols(do_buf, h, DH, DO_ROWS)
        own_k = own_s[h, 0:DH, :].astype(F32) * (SCALE * LOG2E)
        own_v = own_s[h, DH:2 * DH, :].astype(F32)
        hi = own_k.astype(BF16).astype(F32)
        index = lax.broadcasted_iota(jnp.int32, (16, SUB), 0)
        first = jnp.where(index < 3, 1.0, 0.0)
        second = jnp.where((index >= 3) & (index < 6), 1.0, 0.0)
        zeros = jnp.zeros((48, SUB), F32)
        left_s = jnp.concatenate([hi, own_k - hi, first, zeros, zeros, jnp.zeros((16, SUB), F32)], 0).T.astype(BF16)
        s = nn(left_s[:, :QD_ROWS], jnp.concatenate([q_t, q_t, stats], 0))
        j = lax.broadcasted_iota(jnp.int32, (SUB, 1), 0)
        row = sq * ROWS + (j >> 5) * (RATE * BLK) + ph * BLK + (j & 31)
        probs = jnp.where(row < valid[0], jnp.exp2(s), 0.0).astype(BF16)
        left_d = jnp.concatenate([own_v, second, zeros], 0).T.astype(BF16)
        dprob = nn(left_d[:, :DH + 16], jnp.concatenate([do_t, stats], 0))
        dscore = dprob.astype(BF16) * probs
        return jnp.concatenate([nt(dscore, q_t) * SCALE, nt(probs, do_t)], 1).T

    outs = []

    def finish(n, near, far, out, dest):
        for h in range(HEADS):
            parts = place_parts(far[h], phases[h])
            for c in range(16):
                cols = pl.ds(c * 128, 128)
                placed = jnp.where(place_mask(phases[h], c), parts[c // 4], 0.0)
                out[h, :, cols] = (near[h, :, cols].astype(F32) + placed).astype(BF16)
        outs.append(pltpu.make_async_copy(out, dest.at[0], out_sem.at[n]))
        outs[-1].start()

    for c in copies[:5]:
        c.wait()
    finish(0, aq_s, fq_s, oq_s, dq_hbm)
    both = [far_backward_kv(h) for h in range(HEADS)]
    for c in copies[5:]:
        c.wait()
    finish(1, ak_s, [b[:DH] for b in both], ok_s, dk_hbm)
    half, quarter, wide = HEADS * DH // 2, HEADS * DH // 4, D // 2
    for cc in range(2):
        for t in range(4):
            gw_s[cc * half + (t // 2) * quarter:cc * half + (t // 2 + 1) * quarter, (t % 2) * wide:(t % 2 + 1) * wide] = (
                d_buf[cc, t].astype(F32))
    outs.append(pltpu.make_async_copy(gw_s, gw_hbm, out_sem.at[3]))
    outs[-1].start()
    finish(2, av_s, [b[DH:] for b in both], ov_s, dv_hbm)
    for c in outs:
        c.wait()


def shards(queries, key_states, value_states, out_weight, grad_output, phases, valid_rows):
    big = lambda dtype: pltpu.VMEM((HEADS, DH, ROWS), dtype)
    dma = pltpu.SemaphoreType.DMA
    any_spec = pl.BlockSpec(memory_space=pl.ANY)
    smem = pl.BlockSpec(memory_space=pltpu.SMEM)
    chunk = (HEADS * DH // 4, D // 2)
    state = jax.ShapeDtypeStruct(queries.shape, BF16)
    near = jax.ShapeDtypeStruct((HEADS, DH, ROWS), BF16)
    shape = jax.ShapeDtypeStruct
    passed = [
        near, near, near, shape((HEADS, DH, SUB), F32), shape((HEADS, 2 * DH, SUB), BF16),
        shape((2, 8, HEADS, DH, SUB), BF16), shape((2, 8, HEADS, DO_ROWS, SUB), BF16), shape((2, 4, *chunk), BF16)]
    between = pl.pallas_call(
        front_kernel,
        out_shape=passed,
        in_specs=[smem, smem] + [any_spec] * 5,
        out_specs=[any_spec] * 8,
        scratch_shapes=[
            big(BF16), big(BF16), big(BF16),
            pltpu.VMEM((HEADS * DH, D), BF16), pltpu.VMEM((ROWS, D), BF16),
            big(BF16),
            pltpu.VMEM((2 * HEADS, SEG, SEG), BF16), pltpu.VMEM((SEG, SEG), BF16),
            big(F32), pltpu.VMEM((HEADS, 8, ROWS), F32), big(BF16), big(BF16),
            pltpu.VMEM((2, HEADS, 8, 2 * DH, SUB), BF16),
            pltpu.VMEM((HEADS, DH, SUB), BF16), pltpu.VMEM((HEADS, DO_ROWS, SUB), BF16),
            pltpu.VMEM((HEADS, SUB, SPAN), BF16), pltpu.VMEM((HEADS, DH, SUB), F32), pltpu.VMEM((HEADS, DH + 8, SUB), F32),
            big(BF16), big(BF16), big(BF16),
            pltpu.VMEM((HEADS * DH, D), F32),
            pltpu.VMEM((HEADS * DH // 2, D), BF16), pltpu.VMEM((HEADS * DH // 2, D), BF16),
            pltpu.VMEM((HEADS * DH // 2, D), F32),
            pltpu.VMEM((4, *chunk), BF16), pltpu.VMEM((4, *chunk), BF16), pltpu.VMEM((4, *chunk), BF16),
            pltpu.VMEM(chunk, BF16),
            dma((5,)), dma((3, HEADS)), dma((7,)), dma((21,)), dma((21,)), dma((28,)), dma((28,)), dma((5,)), dma((5,)),
            dma((2,)), dma((3,)), dma((3,)), dma((3,)), dma((3,)), dma((7,)), dma((7,)),
        ],
        compiler_params=pltpu.CompilerParams(
            collective_id=0, has_side_effects=True, vmem_limit_bytes=58 << 20),
        name="front",
    )(phases, valid_rows, queries, key_states, value_states, out_weight, grad_output)
    return pl.pallas_call(
        back_kernel,
        out_shape=[state, state, state, shape((HEADS * DH, D), F32)],
        in_specs=[smem, smem] + [any_spec] * 8,
        out_specs=[any_spec] * 4,
        scratch_shapes=[pltpu.VMEM(p.shape, p.dtype) for p in passed] + [
            big(BF16), big(BF16), big(BF16), pltpu.VMEM((HEADS * DH, D), F32), dma((8,)), dma((4,))],
        compiler_params=pltpu.CompilerParams(vmem_limit_bytes=58 << 20),
        name="back",
    )(phases, valid_rows, *between)


def solution(mesh):
    heads = P("dp", "tensor", None, "seq")
    return jax.shard_map(
        shards, mesh=mesh,
        in_specs=(heads, heads, heads, P("tensor", None), P("dp", "seq", None), P("tensor"), P("dp")),
        out_specs=(heads, heads, heads, P("tensor", None)),
        check_vma=False,
    )
```

```python
import jax
import jax.numpy as jnp
from jax import lax
from jax.experimental import pallas as pl
from jax.experimental.pallas import tpu as pltpu
from jax.sharding import PartitionSpec as P

F32 = jnp.float32
BF16 = jnp.bfloat16
SEG = 1024
RATE = 16
BLK = 32
HEADS = 3
DH = 64
ROWS = 2048
SUB = ROWS // RATE
D = 768
PEERS = 16
SPAN = PEERS * SUB
SCALE = 0.125
LOG2E = 1.4426950408889634
DO_ROWS = 80
QD_ROWS = DH + DO_ROWS
MESH = pl.DeviceIdType.MESH


def nn(a, b):
    return jnp.dot(a, b, preferred_element_type=F32)


def nt(a, b):
    return lax.dot_general(a, b, (((1,), (1,)), ((), ())), preferred_element_type=F32)


def hi_lo(x):
    hi = x.astype(BF16)
    return hi, (x - hi.astype(F32)).astype(BF16)


def split3(x):
    hi = x.astype(BF16)
    rest = x - hi.astype(F32)
    mid = rest.astype(BF16)
    return hi, mid, (rest - mid.astype(F32)).astype(BF16)


def lanes(n=SUB):
    return lax.broadcasted_iota(jnp.int32, (1, n), 1)


def turn(x, groups):
    groups = groups % 4
    return x if groups == 0 else pltpu.roll(x, groups * 32, 1)


def choose(options, which):
    out = options[0]
    for n in range(1, len(options)):
        out = jnp.where(which == n, options[n], out)
    return out


def pick(load, phase):
    chunk = jnp.full((1, SUB), phase >> 2, jnp.int32)
    part = jnp.full((1, SUB), phase & 3, jnp.int32)
    group = lanes() >> 5
    out = None
    for b in range(4):
        x = choose([load(b * 512 + n * 128).astype(F32) for n in range(4)], chunk)
        x = choose([turn(x, b - n) for n in range(4)], part)
        out = x if b == 0 else jnp.where(group == b, x, out)
    return out


def place_parts(x, phase):
    part = jnp.full((1, SUB), phase & 3, jnp.int32)
    turned = [turn(x, n) for n in range(4)]
    return [choose([turned[(n - b) % 4] for n in range(4)], part) for b in range(4)]


def place_mask(phase, c):
    want = jnp.where((phase >> 2) == (c % 4), phase & 3, -1)
    return (lanes() >> 5) == want


def front_kernel(
    phases, valid, q_hbm, k_hbm, v_hbm, w_hbm, go_hbm,
    aq_hbm, ak_hbm, av_hbm, fq_hbm, own_hbm, q_far, do_far, d_far,
    q_s, k_s, v_s, w_s, go_s, g_s, e_s, ds_s, on_s, st_s, nd_s, at_s,
    kv_buf, q_own, do_own, gp_s, fe_s, fq_s, fr_s, aq_s, ak_s, av_s,
    gw_s, a_send, a_recv, half_s, b_send, b_recv, c_buf, d_own,
    in_sem, out_sem, own_sem, kv_send, kv_recv, qd_send, qd_recv, pair_send, pair_recv,
    a_sem, b_ss, b_rs, c_ss, c_rs, d_ss, d_rs,
):
    dp, sq, tz = lax.axis_index("dp"), lax.axis_index("seq"), lax.axis_index("tensor")
    y, x, core = sq // 8, (sq % 8) // 2, sq % 2
    yx = sq // 2
    yg = dp * 2 + y

    copies = [
        pltpu.make_async_copy(k_hbm.at[0], k_s, in_sem.at[0]),
        pltpu.make_async_copy(v_hbm.at[0], v_s, in_sem.at[1]),
        pltpu.make_async_copy(q_hbm.at[0], q_s, in_sem.at[2]),
        pltpu.make_async_copy(w_hbm, w_s, in_sem.at[3]),
        pltpu.make_async_copy(go_hbm.at[0], go_s, in_sem.at[4]),
    ]
    for c in copies:
        c.start()

    def at_yx(k):
        yy, xx = (y + k // 4) % 2, (x + k % 4) % 4
        return yy * 4 + xx

    def from_yx(k):
        yy, xx = (y + 2 - k // 4) % 2, (x + 4 - k % 4) % 4
        return yy * 4 + xx

    same_core = [(dp, at_yx(k) * 2 + core, tz) for k in range(1, 8)]
    sibling = (dp, yx * 2 + 1 - core, tz)
    other_core = [(dp, (y * 4 + (x + k) % 4) * 2 + 1 - core, tz) for k in range(1, 4)]
    y_peers = []
    for k in range(1, 4):
        there = (yg + k) % 4
        y_peers.append((there // 2, (there % 2) * 8 + x * 2 + core, tz))
    barrier = pltpu.get_barrier_semaphore()
    dp_peers = [(1 - dp, yy * 8 + x * 2 + core, tz) for yy in range(2)]
    greet = same_core + [sibling] + other_core + dp_peers
    for peer in greet:
        pl.semaphore_signal(barrier, inc=1, device_id=peer, device_id_type=MESH)

    for c in copies[:2]:
        c.wait()
    for h in range(HEADS):
        ph = phases[h]
        kv_buf[core, 0, yx, h] = pick(lambda o: k_s[h, :, pl.ds(o, 128)], ph).astype(BF16)
        kv_buf[core, 1, yx, h] = pick(lambda o: v_s[h, :, pl.ds(o, 128)], ph).astype(BF16)
    pl.semaphore_wait(barrier, len(greet))

    def gather(mine, slot, ss, rs, base):
        sends, recvs = [], []
        for k in range(1, 8):
            n = base + k - 1
            sends.append(pltpu.make_async_remote_copy(
                mine, slot(yx), ss.at[n], rs.at[n], device_id=same_core[k - 1], device_id_type=MESH))
            recvs.append(pltpu.make_async_remote_copy(
                mine, slot(from_yx(k)), ss.at[n], rs.at[n], device_id=same_core[k - 1], device_id_type=MESH))
        return sends, recvs

    def to_pair(buf, i):
        out = pltpu.make_async_remote_copy(
            buf(core), buf(core), pair_send.at[i], pair_recv.at[i], device_id=sibling, device_id_type=MESH)
        back = pltpu.make_async_remote_copy(
            buf(1 - core), buf(1 - core), pair_send.at[i], pair_recv.at[i], device_id=sibling, device_id_type=MESH)
        return out, back

    kv_out, kv_in, kv_pair = [], [], []
    for t in range(2):
        sends, recvs = gather(kv_buf.at[core, t, yx], lambda n, t=t: kv_buf.at[core, t, n], kv_send, kv_recv, 7 * t)
        kv_out.append(sends)
        kv_in.append(recvs)
        kv_pair.append(to_pair(lambda c, t=t: kv_buf.at[c, t], t))
        for c in sends:
            c.start()

    copies[2].wait()
    for h in range(HEADS):
        q_own[h] = pick(lambda o: q_s[h, :, pl.ds(o, 128)], phases[h]).astype(BF16)
    own_copies = [
        pltpu.make_async_copy(kv_buf.at[core, t, yx], own_hbm.at[t], own_sem.at[t]) for t in range(2)]
    own_copies.append(pltpu.make_async_copy(q_own, q_far.at[core, yx], own_sem.at[3]))
    for c in own_copies:
        c.start()

    def forward_pair(h):
        for c in kv_in[h]:
            c.wait_recv()
        kv_pair[h][0].start()

    def near_forward(u, carry):
        h, off = u // 2, pl.multiple_of((u % 2) * SEG, SEG)
        rows = pl.ds(off, SEG)
        k_t, v_t = k_s[h, :, rows], v_s[h, :, rows]
        qh, ql = hi_lo(q_s[h, :, rows].astype(F32) * (SCALE * LOG2E))
        kk = jnp.concatenate([k_t, k_t], 0).T
        s = nn(kk, jnp.concatenate([qh, ql], 0))
        m = jnp.max(s, axis=0, keepdims=True)
        e = jnp.exp2(s - m).astype(BF16)
        e_s[u] = e
        o = nn(jnp.concatenate([v_t, jnp.ones((16, SEG), BF16)], 0), e)
        total = o[DH:DH + 1]
        r = 1.0 / total
        on_s[h, :, rows] = o[:DH] * r
        st_s[h, 0:1, rows] = r
        st_s[h, 1:2, rows] = m + jnp.log2(total)
        return carry

    for u in range(2 * HEADS):
        near_forward(u, 0)
    forward_pair(0)
    copies[3].wait()
    copies[4].wait()
    g_s[...] = nt(w_s[...], go_s[...]).astype(BF16).reshape(HEADS, DH, ROWS)
    for h in range(HEADS):
        for c in range(16):
            cols = pl.ds(c * 128, 128)
            near = on_s[h, :, cols]
            rr = st_s[h, 0:1, cols]
            nd = (g_s[h, :, cols].astype(F32) * rr).astype(BF16)
            nd_s[h, :, cols] = nd
            st_s[h, 2:3, cols] = -jnp.sum(nd.astype(F32) * near, axis=0, keepdims=True)
            at_s[h, :, cols] = jnp.where(place_mask(phases[h], c), 0.0, near).astype(BF16)
    forward_pair(1)
    gw_s[...] = nn(at_s[...].reshape(HEADS * DH, ROWS), go_s[...])
    q_out, q_in = gather(q_own, lambda n: q_far.at[core, n], qd_send, qd_recv, 0)
    q_pair = to_pair(lambda c: q_far.at[c], HEADS)
    for c in q_out:
        c.start()

    for h in range(HEADS):
        which = jnp.full((1, D), phases[h], jnp.int32)
        for b in range(4):
            rows = [go_s[b * 512 + n * BLK:b * 512 + (n + 1) * BLK, :] for n in range(RATE)]
            gp_s[h, b * BLK:(b + 1) * BLK, :] = choose(rows, which)

    key_index = lanes(SPAN)

    def all_cols(t, h):
        return jnp.concatenate([kv_buf[n % 2, t, n // 2, h] for n in range(PEERS)], 1)

    def far_scores(h):
        ph = phases[h]
        k_t = all_cols(0, h)
        q_t = q_own[h].astype(F32) * (SCALE * LOG2E)
        hi = q_t.astype(BF16).astype(F32)
        lhs = jnp.concatenate([hi, q_t - hi], 0).T.astype(BF16)
        s = nn(lhs, jnp.concatenate([k_t, k_t], 0))
        row = (key_index >> 5) * (RATE * BLK) + ph * BLK + (key_index & 31)
        s = jnp.where(row < valid[0], s, -1e30)
        m = jnp.max(s, axis=1, keepdims=True)
        e = jnp.exp2(s - m).astype(BF16)
        fe_s[h] = e
        return m

    def far_forward(h, m):
        ph = phases[h]
        e, v_t = fe_s[h], all_cols(1, h)
        o = nt(e, jnp.concatenate([v_t, jnp.ones((16, SPAN), BF16)], 0))
        total = o[:, DH:DH + 1]
        r = 1.0 / total
        packed = jnp.concatenate(
            [o[:, :DH] * r, jnp.broadcast_to(m + jnp.log2(total), (SUB, 32)), jnp.broadcast_to(r, (SUB, 32))], 1).T
        far_out, far_lse, far_r = packed[0:DH], packed[DH:DH + 1], packed[96:97]
        near_out = pick(lambda o: on_s[h, :, pl.ds(o, 128)], ph)
        near_stats = pick(lambda o: st_s[h, :, pl.ds(o, 128)], ph)
        near_r, near_lse = near_stats[0:1], near_stats[1:2]
        g = pick(lambda o: g_s[h, :, pl.ds(o, 128)], ph)
        mixing = 1.0 / (1.0 + jnp.exp2(near_lse - far_lse))
        rest = 1.0 / (1.0 + jnp.exp2(far_lse - near_lse))
        diff = far_out - near_out
        comb = near_out + mixing * diff
        far_dlse = jnp.sum(g * diff, axis=0, keepdims=True) * mixing * rest
        far_dout = (mixing * g).astype(BF16)
        fd = far_dout.astype(F32)
        term = far_dlse - jnp.sum(fd * far_out, axis=0, keepdims=True)
        do_own[h, 0:DH, :] = far_dout
        do_own[h, DH:DO_ROWS, :] = jnp.concatenate(
            [*split3(-far_lse), *split3(term), jnp.zeros((10, SUB), BF16)], 0)
        scaled = (fd * far_r).astype(BF16).astype(F32)
        term_r = far_dlse * far_r - jnp.sum(scaled * far_out, axis=0, keepdims=True)
        fr_s[h, 0:DH, :] = scaled
        fr_s[h, DH:DH + 8, :] = jnp.broadcast_to(term_r, (8, SUB))
        gw_s[h * DH:(h + 1) * DH, :] += nn(comb.astype(BF16), gp_s[h])
        near_dout = (rest * g).astype(BF16).astype(F32)
        nd = (near_dout * near_r).astype(BF16).astype(F32)
        near_term = -far_dlse * near_r - jnp.sum(nd * near_out, axis=0, keepdims=True)
        parts = place_parts(jnp.concatenate([nd, near_term, jnp.zeros((7, SUB), F32)], 0), ph)
        for c in range(16):
            cols = pl.ds(c * 128, 128)
            mask = place_mask(ph, c)
            part = parts[c // 4]
            nd_s[h, :, cols] = jnp.where(mask, part[:DH], nd_s[h, :, cols].astype(F32)).astype(BF16)
            st_s[h, 2:3, cols] = jnp.where(mask, part[DH:DH + 1], st_s[h, 2:3, cols])

    kv_pair[0][1].wait_recv()
    tops = [far_scores(h) for h in range(HEADS)]
    kv_pair[1][1].wait_recv()
    for h in range(HEADS):
        far_forward(h, tops[h])

    do_out, do_in = [], []
    for h in range(HEADS):
        sends, recvs = gather(do_own.at[h], lambda n, h=h: do_far.at[core, n, h], qd_send, qd_recv, 7 + 7 * h)
        do_out += sends
        do_in += recvs
    do_pair = to_pair(lambda c: do_far.at[c], HEADS + 1)
    for c in do_out[:14]:
        c.start()
    do_copy = pltpu.make_async_copy(do_own, do_far.at[core, yx], own_sem.at[4])
    do_copy.start()

    half = HEADS * DH // 2
    a_send[...] = gw_s[pl.ds(pl.multiple_of((1 - core) * half, 32), half), :].astype(BF16)
    a_copy = pltpu.make_async_remote_copy(a_send, a_recv, a_sem.at[0], a_sem.at[1], device_id=sibling, device_id_type=MESH)
    a_copy.start()

    def far_backward_q(h, carry):
        k_t, v_t = all_cols(0, h), all_cols(1, h)
        d = fr_s[h]
        term = d[DH:DH + 1]
        term_hi = term.astype(BF16).astype(F32)
        left = jnp.concatenate([d[:DH], term_hi, term - term_hi, jnp.zeros((62, SUB), F32)], 0).T.astype(BF16)
        ones = jnp.concatenate([jnp.ones((2, SPAN), BF16), jnp.zeros((62, SPAN), BF16)], 0)
        dprob = nn(left, jnp.concatenate([v_t, ones], 0))
        dscore = dprob.astype(BF16) * fe_s[h]
        fq_s[h] = nt(dscore, k_t).T * SCALE
        return carry

    for h in range(HEADS):
        far_backward_q(h, 0)
    fq_copy = pltpu.make_async_copy(fq_s, fq_hbm, own_sem.at[5])
    fq_copy.start()

    quarter, wide = half // 2, D // 2
    b_out, b_in = [], []
    for k in range(1, 4):
        b_out.append(pltpu.make_async_remote_copy(
            b_send.at[(x + k) % 4], b_recv.at[x], b_ss.at[k - 1], b_rs.at[k - 1],
            device_id=same_core[k - 1], device_id_type=MESH))
        b_in.append(pltpu.make_async_remote_copy(
            b_send.at[(x + k) % 4], b_recv.at[(x + 4 - k) % 4], b_ss.at[k - 1], b_rs.at[k - 1],
            device_id=same_core[k - 1], device_id_type=MESH))
    c_out, c_in = [], []
    for k in range(1, 4):
        c_out.append(pltpu.make_async_remote_copy(
            c_buf.at[yg], c_buf.at[yg], c_ss.at[k - 1], c_rs.at[k - 1], device_id=y_peers[k - 1], device_id_type=MESH))
        there = (yg + 4 - k) % 4
        c_in.append(pltpu.make_async_remote_copy(
            c_buf.at[there], c_buf.at[there], c_ss.at[k - 1], c_rs.at[k - 1], device_id=y_peers[k - 1], device_id_type=MESH))
    d_out, d_in = [], []
    d_peers = [same_core[k - 1] for k in range(1, 4)] + [sibling] + other_core
    for k in range(1, 8):
        d_out.append(pltpu.make_async_remote_copy(
            d_own, d_far.at[core, x], d_ss.at[k - 1], d_rs.at[k - 1], device_id=d_peers[k - 1], device_id_type=MESH))
        theirs = d_far.at[core if k < 4 else 1 - core, (x + 4 - k % 4) % 4]
        d_in.append(pltpu.make_async_remote_copy(
            d_own, theirs, d_ss.at[k - 1], d_rs.at[k - 1], device_id=d_peers[k - 1], device_id_type=MESH))
    d_copy = pltpu.make_async_copy(d_own, d_far.at[core, x], own_sem.at[6])

    def outs(h):
        return [
            pltpu.make_async_copy(aq_s.at[h], aq_hbm.at[h], out_sem.at[0, h]),
            pltpu.make_async_copy(ak_s.at[h], ak_hbm.at[h], out_sem.at[1, h]),
            pltpu.make_async_copy(av_s.at[h], av_hbm.at[h], out_sem.at[2, h]),
        ]


    def near_backward(u, carry):
        h, off = u // 2, pl.multiple_of((u % 2) * SEG, SEG)
        rows = pl.ds(off, SEG)
        q_t, k_t, v_t, gh = q_s[h, :, rows], k_s[h, :, rows], v_s[h, :, rows], nd_s[h, :, rows]
        th, tl = hi_lo(st_s[h, 2:3, rows])
        gg = jnp.concatenate([gh, jnp.concatenate([th, tl, jnp.zeros((14, SEG), BF16)], 0)], 0)
        vv = jnp.concatenate([v_t, jnp.ones((2, SEG), BF16), jnp.zeros((14, SEG), BF16)], 0).T
        for ib in range(2):
            cols = slice(ib * 512, ib * 512 + 512)
            dprob = nn(vv, gg[:, cols])
            ds = dprob.astype(BF16) * e_s[u, :, cols]
            ds_s[:, cols] = ds
            aq_s[h, :, pl.ds(pl.multiple_of(off + ib * 512, 512), 512)] = (nn(k_t, ds) * SCALE).astype(BF16)
        for jb in range(2):
            cols = slice(jb * 512, jb * 512 + 512)
            out_cols = pl.ds(pl.multiple_of(off + jb * 512, 512), 512)
            ak_s[h, :, out_cols] = (nt(ds_s[cols, :], q_t).T * SCALE).astype(BF16)
            av_s[h, :, out_cols] = nt(e_s[u, cols, :], gh).T.astype(BF16)

        @pl.when(u % 2 == 1)
        def _():
            for c in outs(h):
                c.start()

        @pl.when(u == 0)
        def _():
            for c in own_copies:
                c.wait()
            for c in q_in:
                c.wait_recv()
            q_pair[0].start()
            a_copy.wait()
            mine = gw_s[pl.ds(pl.multiple_of(core * half, 32), half), :]
            half_s[...] = mine + a_recv[...].astype(F32)
            for t in range(4):
                b_send[t] = half_s[(t // 2) * quarter:(t // 2 + 1) * quarter, (t % 2) * wide:(t % 2 + 1) * wide].astype(BF16)
            for c in b_out + do_out[14:]:
                c.start()

        @pl.when(u == 1)
        def _():
            for c in b_in:
                c.wait_recv()
            b_recv[x] = b_send[x]
            total = b_recv[0].astype(F32)
            for t in range(1, 4):
                total = total + b_recv[t].astype(F32)
            c_buf[yg] = total.astype(BF16)
            for c in c_out:
                c.start()

        @pl.when(u == 3)
        def _():
            for c in c_in:
                c.wait_recv()
            total = c_buf[0].astype(F32)
            for t in range(1, 4):
                total = total + c_buf[t].astype(F32)
            d_own[...] = total.astype(BF16)
            for c in d_out:
                c.start()
            d_copy.start()

        @pl.when(u == 4)
        def _():
            for c in do_in:
                c.wait_recv()
            do_copy.wait()
            do_pair[0].start()

        return carry

    lax.fori_loop(0, 2 * HEADS, near_backward, 0)
    fq_copy.wait()
    d_copy.wait()
    for sends in kv_out:
        for c in sends:
            c.wait_send()
    for pair in kv_pair + [q_pair, do_pair]:
        pair[0].wait_send()
    for c in q_out + do_out + b_out + c_out + d_out:
        c.wait_send()
    q_pair[1].wait_recv()
    do_pair[1].wait_recv()
    for c in d_in:
        c.wait_recv()
    for h in range(HEADS):
        for c in outs(h):
            c.wait()


def back_kernel(
    phases, valid, aq_hbm, ak_hbm, av_hbm, fq_hbm, own_hbm, q_far, do_far, d_far,
    dq_hbm, dk_hbm, dv_hbm, gw_hbm,
    aq_s, ak_s, av_s, fq_s, own_s, q_buf, do_buf, d_buf, oq_s, ok_s, ov_s, gw_s, in_sem, out_sem,
):
    sq = lax.axis_index("seq")
    pairs = ((q_far, q_buf), (own_hbm, own_s), (do_far, do_buf), (fq_hbm, fq_s),
             (aq_hbm, aq_s), (ak_hbm, ak_s), (av_hbm, av_s), (d_far, d_buf))
    copies = [pltpu.make_async_copy(a, b, in_sem.at[n]) for n, (a, b) in enumerate(pairs)]
    for c in copies:
        c.start()

    def all_cols(buf, h, lo, hi):
        return jnp.concatenate([buf[n % 2, n // 2, h, lo:hi, :] for n in range(PEERS)], 1)

    def far_backward_kv(h):
        ph = phases[h]
        q_t, do_t = all_cols(q_buf, h, 0, DH), all_cols(do_buf, h, 0, DH)
        stats = all_cols(do_buf, h, DH, DO_ROWS)
        own_k = own_s[0, h].astype(F32) * (SCALE * LOG2E)
        own_v = own_s[1, h].astype(F32)
        hi = own_k.astype(BF16).astype(F32)
        index = lax.broadcasted_iota(jnp.int32, (16, SUB), 0)
        first = jnp.where(index < 3, 1.0, 0.0)
        second = jnp.where((index >= 3) & (index < 6), 1.0, 0.0)
        zeros = jnp.zeros((48, SUB), F32)
        left_s = jnp.concatenate([hi, own_k - hi, first, zeros, zeros, jnp.zeros((16, SUB), F32)], 0).T.astype(BF16)
        s = nn(left_s[:, :QD_ROWS], jnp.concatenate([q_t, q_t, stats], 0))
        j = lax.broadcasted_iota(jnp.int32, (SUB, 1), 0)
        row = sq * ROWS + (j >> 5) * (RATE * BLK) + ph * BLK + (j & 31)
        probs = jnp.where(row < valid[0], jnp.exp2(s), 0.0).astype(BF16)
        left_d = jnp.concatenate([own_v, second, zeros], 0).T.astype(BF16)
        dprob = nn(left_d[:, :DH + 16], jnp.concatenate([do_t, stats], 0))
        dscore = dprob.astype(BF16) * probs
        return jnp.concatenate([nt(dscore, q_t) * SCALE, nt(probs, do_t)], 1).T

    outs = []

    def finish(n, near, far, out, dest):
        for h in range(HEADS):
            parts = place_parts(far[h], phases[h])
            for c in range(16):
                cols = pl.ds(c * 128, 128)
                placed = jnp.where(place_mask(phases[h], c), parts[c // 4], 0.0)
                out[h, :, cols] = (near[h, :, cols].astype(F32) + placed).astype(BF16)
        outs.append(pltpu.make_async_copy(out, dest.at[0], out_sem.at[n]))
        outs[-1].start()

    for c in copies[:5]:
        c.wait()
    finish(0, aq_s, fq_s, oq_s, dq_hbm)
    both = [far_backward_kv(h) for h in range(HEADS)]
    for c in copies[5:]:
        c.wait()
    finish(1, ak_s, [b[:DH] for b in both], ok_s, dk_hbm)
    half, quarter, wide = HEADS * DH // 2, HEADS * DH // 4, D // 2
    for cc in range(2):
        for t in range(4):
            gw_s[cc * half + (t // 2) * quarter:cc * half + (t // 2 + 1) * quarter, (t % 2) * wide:(t % 2 + 1) * wide] = (
                d_buf[cc, t].astype(F32))
    outs.append(pltpu.make_async_copy(gw_s, gw_hbm, out_sem.at[3]))
    outs[-1].start()
    finish(2, av_s, [b[DH:] for b in both], ov_s, dv_hbm)
    for c in outs:
        c.wait()


def shards(queries, key_states, value_states, out_weight, grad_output, phases, valid_rows):
    big = lambda dtype: pltpu.VMEM((HEADS, DH, ROWS), dtype)
    dma = pltpu.SemaphoreType.DMA
    any_spec = pl.BlockSpec(memory_space=pl.ANY)
    smem = pl.BlockSpec(memory_space=pltpu.SMEM)
    chunk = (HEADS * DH // 4, D // 2)
    state = jax.ShapeDtypeStruct(queries.shape, BF16)
    near = jax.ShapeDtypeStruct((HEADS, DH, ROWS), BF16)
    shape = jax.ShapeDtypeStruct
    passed = [
        near, near, near, shape((HEADS, DH, SUB), F32), shape((2, HEADS, DH, SUB), BF16),
        shape((2, 8, HEADS, DH, SUB), BF16), shape((2, 8, HEADS, DO_ROWS, SUB), BF16), shape((2, 4, *chunk), BF16)]
    between = pl.pallas_call(
        front_kernel,
        out_shape=passed,
        in_specs=[smem, smem] + [any_spec] * 5,
        out_specs=[any_spec] * 8,
        scratch_shapes=[
            big(BF16), big(BF16), big(BF16),
            pltpu.VMEM((HEADS * DH, D), BF16), pltpu.VMEM((ROWS, D), BF16),
            big(BF16),
            pltpu.VMEM((2 * HEADS, SEG, SEG), BF16), pltpu.VMEM((SEG, SEG), BF16),
            big(F32), pltpu.VMEM((HEADS, 8, ROWS), F32), big(BF16), big(BF16),
            pltpu.VMEM((2, 2, 8, HEADS, DH, SUB), BF16),
            pltpu.VMEM((HEADS, DH, SUB), BF16), pltpu.VMEM((HEADS, DO_ROWS, SUB), BF16),
            pltpu.VMEM((HEADS, SUB, D), BF16),
            pltpu.VMEM((HEADS, SUB, SPAN), BF16), pltpu.VMEM((HEADS, DH, SUB), F32), pltpu.VMEM((HEADS, DH + 8, SUB), F32),
            big(BF16), big(BF16), big(BF16),
            pltpu.VMEM((HEADS * DH, D), F32),
            pltpu.VMEM((HEADS * DH // 2, D), BF16), pltpu.VMEM((HEADS * DH // 2, D), BF16),
            pltpu.VMEM((HEADS * DH // 2, D), F32),
            pltpu.VMEM((4, *chunk), BF16), pltpu.VMEM((4, *chunk), BF16), pltpu.VMEM((4, *chunk), BF16),
            pltpu.VMEM(chunk, BF16),
            dma((5,)), dma((3, HEADS)), dma((7,)), dma((21,)), dma((21,)), dma((28,)), dma((28,)), dma((5,)), dma((5,)),
            dma((2,)), dma((3,)), dma((3,)), dma((3,)), dma((3,)), dma((7,)), dma((7,)),
        ],
        compiler_params=pltpu.CompilerParams(
            collective_id=0, has_side_effects=True, vmem_limit_bytes=58 << 20),
        name="front",
    )(phases, valid_rows, queries, key_states, value_states, out_weight, grad_output)
    return pl.pallas_call(
        back_kernel,
        out_shape=[state, state, state, shape((HEADS * DH, D), F32)],
        in_specs=[smem, smem] + [any_spec] * 8,
        out_specs=[any_spec] * 4,
        scratch_shapes=[pltpu.VMEM(p.shape, p.dtype) for p in passed] + [
            big(BF16), big(BF16), big(BF16), pltpu.VMEM((HEADS * DH, D), F32), dma((8,)), dma((4,))],
        compiler_params=pltpu.CompilerParams(vmem_limit_bytes=58 << 20),
        name="back",
    )(phases, valid_rows, *between)


def solution(mesh):
    heads = P("dp", "tensor", None, "seq")
    return jax.shard_map(
        shards, mesh=mesh,
        in_specs=(heads, heads, heads, P("tensor", None), P("dp", "seq", None), P("tensor"), P("dp")),
        out_specs=(heads, heads, heads, P("tensor", None)),
        check_vma=False,
    )
```

```python
import jax
import jax.numpy as jnp
from jax import lax
from jax.experimental import pallas as pl
from jax.experimental.pallas import tpu as pltpu
from jax.sharding import PartitionSpec as P

F32 = jnp.float32
BF16 = jnp.bfloat16
SEG = 1024
RATE = 16
BLK = 32
HEADS = 3
DH = 64
ROWS = 2048
SUB = ROWS // RATE
D = 768
PEERS = 16
SPAN = PEERS * SUB
SCALE = 0.125
LOG2E = 1.4426950408889634
DO_ROWS = 80
QD_ROWS = DH + DO_ROWS
MESH = pl.DeviceIdType.MESH


def nn(a, b):
    return jnp.dot(a, b, preferred_element_type=F32)


def nt(a, b):
    return lax.dot_general(a, b, (((1,), (1,)), ((), ())), preferred_element_type=F32)


def hi_lo(x):
    hi = x.astype(BF16)
    return hi, (x - hi.astype(F32)).astype(BF16)


def split3(x):
    hi = x.astype(BF16)
    rest = x - hi.astype(F32)
    mid = rest.astype(BF16)
    return hi, mid, (rest - mid.astype(F32)).astype(BF16)


def lanes(n=SUB):
    return lax.broadcasted_iota(jnp.int32, (1, n), 1)


def turn(x, groups):
    groups = groups % 4
    return x if groups == 0 else pltpu.roll(x, groups * 32, 1)


def choose(options, which):
    out = options[0]
    for n in range(1, len(options)):
        out = jnp.where(which == n, options[n], out)
    return out


def pick(load, phase):
    chunk = jnp.full((1, SUB), phase >> 2, jnp.int32)
    part = jnp.full((1, SUB), phase & 3, jnp.int32)
    group = lanes() >> 5
    out = None
    for b in range(4):
        x = choose([load(b * 512 + n * 128).astype(F32) for n in range(4)], chunk)
        x = choose([turn(x, b - n) for n in range(4)], part)
        out = x if b == 0 else jnp.where(group == b, x, out)
    return out


def place_parts(x, phase):
    part = jnp.full((1, SUB), phase & 3, jnp.int32)
    turned = [turn(x, n) for n in range(4)]
    return [choose([turned[(n - b) % 4] for n in range(4)], part) for b in range(4)]


def place_mask(phase, c):
    want = jnp.where((phase >> 2) == (c % 4), phase & 3, -1)
    return (lanes() >> 5) == want


def front_kernel(
    phases, valid, q_hbm, k_hbm, v_hbm, w_hbm, go_hbm,
    aq_hbm, ak_hbm, av_hbm, fq_hbm, own_hbm, q_far, do_far, d_far,
    q_s, k_s, v_s, w_s, go_s, g_s, e_s, ds_s, on_s, st_s, nd_s, at_s,
    kv_buf, q_own, do_own, gp_s, fe_s, fq_s, fr_s, aq_s, ak_s, av_s,
    gw_s, a_send, a_recv, half_s, b_send, b_recv, c_buf, d_own,
    in_sem, out_sem, own_sem, kv_send, kv_recv, qd_send, qd_recv, pair_send, pair_recv,
    a_sem, b_ss, b_rs, c_ss, c_rs, d_ss, d_rs,
):
    dp, sq, tz = lax.axis_index("dp"), lax.axis_index("seq"), lax.axis_index("tensor")
    y, x, core = sq // 8, (sq % 8) // 2, sq % 2
    yx = sq // 2
    yg = dp * 2 + y

    copies = [
        pltpu.make_async_copy(k_hbm.at[0], k_s, in_sem.at[0]),
        pltpu.make_async_copy(v_hbm.at[0], v_s, in_sem.at[1]),
        pltpu.make_async_copy(q_hbm.at[0], q_s, in_sem.at[2]),
        pltpu.make_async_copy(w_hbm, w_s, in_sem.at[3]),
        pltpu.make_async_copy(go_hbm.at[0], go_s, in_sem.at[4]),
    ]
    for c in copies:
        c.start()

    def at_yx(k):
        yy, xx = (y + k // 4) % 2, (x + k % 4) % 4
        return yy * 4 + xx

    def from_yx(k):
        yy, xx = (y + 2 - k // 4) % 2, (x + 4 - k % 4) % 4
        return yy * 4 + xx

    same_core = [(dp, at_yx(k) * 2 + core, tz) for k in range(1, 8)]
    sibling = (dp, yx * 2 + 1 - core, tz)
    other_core = [(dp, (y * 4 + (x + k) % 4) * 2 + 1 - core, tz) for k in range(1, 4)]
    y_peers = []
    for k in range(1, 4):
        there = (yg + k) % 4
        y_peers.append((there // 2, (there % 2) * 8 + x * 2 + core, tz))
    barrier = pltpu.get_barrier_semaphore()
    dp_peers = [(1 - dp, yy * 8 + x * 2 + core, tz) for yy in range(2)]
    greet = same_core + [sibling] + other_core + dp_peers
    for peer in greet:
        pl.semaphore_signal(barrier, inc=1, device_id=peer, device_id_type=MESH)

    def pick_into(t, ref):
        copies[t].wait()
        for h in range(HEADS):
            kv_buf[core, t, yx, h] = pick(lambda o: ref[h, :, pl.ds(o, 128)], phases[h]).astype(BF16)

    pick_into(0, k_s)
    pl.semaphore_wait(barrier, len(greet))

    def gather(mine, slot, ss, rs, base):
        sends, recvs = [], []
        for k in (6, 2, 5, 7, 1, 3, 4):
            n = base + k - 1
            sends.append(pltpu.make_async_remote_copy(
                mine, slot(yx), ss.at[n], rs.at[n], device_id=same_core[k - 1], device_id_type=MESH))
            recvs.append(pltpu.make_async_remote_copy(
                mine, slot(from_yx(k)), ss.at[n], rs.at[n], device_id=same_core[k - 1], device_id_type=MESH))
        return sends, recvs

    def to_pair(buf, i):
        out = pltpu.make_async_remote_copy(
            buf(core), buf(core), pair_send.at[i], pair_recv.at[i], device_id=sibling, device_id_type=MESH)
        back = pltpu.make_async_remote_copy(
            buf(1 - core), buf(1 - core), pair_send.at[i], pair_recv.at[i], device_id=sibling, device_id_type=MESH)
        return out, back

    kv_out, kv_in, kv_pair = [], [], []
    for t in range(2):
        if t == 1:
            pick_into(1, v_s)
        sends, recvs = gather(kv_buf.at[core, t, yx], lambda n, t=t: kv_buf.at[core, t, n], kv_send, kv_recv, 7 * t)
        kv_out.append(sends)
        kv_in.append(recvs)
        kv_pair.append(to_pair(lambda c, t=t: kv_buf.at[c, t], t))
        for c in sends:
            c.start()

    copies[2].wait()
    for h in range(HEADS):
        q_own[h] = pick(lambda o: q_s[h, :, pl.ds(o, 128)], phases[h]).astype(BF16)
    own_copies = [
        pltpu.make_async_copy(kv_buf.at[core, t, yx], own_hbm.at[t], own_sem.at[t]) for t in range(2)]
    own_copies.append(pltpu.make_async_copy(q_own, q_far.at[core, yx], own_sem.at[3]))
    for c in own_copies:
        c.start()

    def forward_pair(h):
        for c in kv_in[h]:
            c.wait_recv()
        kv_pair[h][0].start()

    def near_forward(u, carry):
        h, off = u // 2, pl.multiple_of((u % 2) * SEG, SEG)
        rows = pl.ds(off, SEG)
        k_t, v_t = k_s[h, :, rows], v_s[h, :, rows]
        qh, ql = hi_lo(q_s[h, :, rows].astype(F32) * (SCALE * LOG2E))
        kk = jnp.concatenate([k_t, k_t], 0).T
        s = nn(kk, jnp.concatenate([qh, ql], 0))
        m = jnp.max(s, axis=0, keepdims=True)
        e = jnp.exp2(s - m).astype(BF16)
        e_s[u] = e
        o = nn(jnp.concatenate([v_t, jnp.ones((16, SEG), BF16)], 0), e)
        total = o[DH:DH + 1]
        r = 1.0 / total
        on_s[h, :, rows] = o[:DH] * r
        st_s[h, 0:1, rows] = r
        st_s[h, 1:2, rows] = m + jnp.log2(total)
        return carry

    for u in range(2 * HEADS):
        near_forward(u, 0)
    forward_pair(0)
    copies[3].wait()
    copies[4].wait()
    g_s[...] = nt(w_s[...], go_s[...]).astype(BF16).reshape(HEADS, DH, ROWS)
    for h in range(HEADS):
        for c in range(16):
            cols = pl.ds(c * 128, 128)
            near = on_s[h, :, cols]
            rr = st_s[h, 0:1, cols]
            nd = (g_s[h, :, cols].astype(F32) * rr).astype(BF16)
            nd_s[h, :, cols] = nd
            st_s[h, 2:3, cols] = -jnp.sum(nd.astype(F32) * near, axis=0, keepdims=True)
            at_s[h, :, cols] = jnp.where(place_mask(phases[h], c), 0.0, near).astype(BF16)
    forward_pair(1)
    gw_s[...] = nn(at_s[...].reshape(HEADS * DH, ROWS), go_s[...])
    q_out, q_in = gather(q_own, lambda n: q_far.at[core, n], qd_send, qd_recv, 0)
    q_pair = to_pair(lambda c: q_far.at[c], HEADS)
    for c in q_out:
        c.start()

    for h in range(HEADS):
        which = jnp.full((1, D), phases[h], jnp.int32)
        for b in range(4):
            rows = [go_s[b * 512 + n * BLK:b * 512 + (n + 1) * BLK, :] for n in range(RATE)]
            gp_s[h, b * BLK:(b + 1) * BLK, :] = choose(rows, which)

    key_index = lanes(SPAN)

    def all_cols(t, h):
        return jnp.concatenate([kv_buf[n % 2, t, n // 2, h] for n in range(PEERS)], 1)

    def far_scores(h):
        ph = phases[h]
        k_t = all_cols(0, h)
        q_t = q_own[h].astype(F32) * (SCALE * LOG2E)
        hi = q_t.astype(BF16).astype(F32)
        lhs = jnp.concatenate([hi, q_t - hi], 0).T.astype(BF16)
        s = nn(lhs, jnp.concatenate([k_t, k_t], 0))
        row = (key_index >> 5) * (RATE * BLK) + ph * BLK + (key_index & 31)
        s = jnp.where(row < valid[0], s, -1e30)
        m = jnp.max(s, axis=1, keepdims=True)
        e = jnp.exp2(s - m).astype(BF16)
        fe_s[h] = e
        return m

    def far_forward(h, m):
        ph = phases[h]
        e, v_t = fe_s[h], all_cols(1, h)
        o = nt(e, jnp.concatenate([v_t, jnp.ones((16, SPAN), BF16)], 0))
        total = o[:, DH:DH + 1]
        r = 1.0 / total
        packed = jnp.concatenate(
            [o[:, :DH] * r, jnp.broadcast_to(m + jnp.log2(total), (SUB, 32)), jnp.broadcast_to(r, (SUB, 32))], 1).T
        far_out, far_lse, far_r = packed[0:DH], packed[DH:DH + 1], packed[96:97]
        near_out = pick(lambda o: on_s[h, :, pl.ds(o, 128)], ph)
        near_stats = pick(lambda o: st_s[h, :, pl.ds(o, 128)], ph)
        near_r, near_lse = near_stats[0:1], near_stats[1:2]
        g = pick(lambda o: g_s[h, :, pl.ds(o, 128)], ph)
        mixing = 1.0 / (1.0 + jnp.exp2(near_lse - far_lse))
        rest = 1.0 / (1.0 + jnp.exp2(far_lse - near_lse))
        diff = far_out - near_out
        comb = near_out + mixing * diff
        far_dlse = jnp.sum(g * diff, axis=0, keepdims=True) * mixing * rest
        far_dout = (mixing * g).astype(BF16)
        fd = far_dout.astype(F32)
        term = far_dlse - jnp.sum(fd * far_out, axis=0, keepdims=True)
        do_own[h, 0:DH, :] = far_dout
        do_own[h, DH:DO_ROWS, :] = jnp.concatenate(
            [*split3(-far_lse), *split3(term), jnp.zeros((10, SUB), BF16)], 0)
        scaled = (fd * far_r).astype(BF16).astype(F32)
        term_r = far_dlse * far_r - jnp.sum(scaled * far_out, axis=0, keepdims=True)
        fr_s[h, 0:DH, :] = scaled
        fr_s[h, DH:DH + 8, :] = jnp.broadcast_to(term_r, (8, SUB))
        gw_s[h * DH:(h + 1) * DH, :] += nn(comb.astype(BF16), gp_s[h])
        near_dout = (rest * g).astype(BF16).astype(F32)
        nd = (near_dout * near_r).astype(BF16).astype(F32)
        near_term = -far_dlse * near_r - jnp.sum(nd * near_out, axis=0, keepdims=True)
        parts = place_parts(jnp.concatenate([nd, near_term, jnp.zeros((7, SUB), F32)], 0), ph)
        for c in range(16):
            cols = pl.ds(c * 128, 128)
            mask = place_mask(ph, c)
            part = parts[c // 4]
            nd_s[h, :, cols] = jnp.where(mask, part[:DH], nd_s[h, :, cols].astype(F32)).astype(BF16)
            st_s[h, 2:3, cols] = jnp.where(mask, part[DH:DH + 1], st_s[h, 2:3, cols])

    kv_pair[0][1].wait_recv()
    tops = [far_scores(h) for h in range(HEADS)]
    kv_pair[1][1].wait_recv()
    for h in range(HEADS):
        far_forward(h, tops[h])

    do_out, do_in = [], []
    for h in range(HEADS):
        sends, recvs = gather(do_own.at[h], lambda n, h=h: do_far.at[core, n, h], qd_send, qd_recv, 7 + 7 * h)
        do_out += sends
        do_in += recvs
    do_pair = to_pair(lambda c: do_far.at[c], HEADS + 1)
    for c in do_out[:14]:
        c.start()
    do_copy = pltpu.make_async_copy(do_own, do_far.at[core, yx], own_sem.at[4])
    do_copy.start()

    half = HEADS * DH // 2
    a_send[...] = gw_s[pl.ds(pl.multiple_of((1 - core) * half, 32), half), :].astype(BF16)
    a_copy = pltpu.make_async_remote_copy(a_send, a_recv, a_sem.at[0], a_sem.at[1], device_id=sibling, device_id_type=MESH)
    a_copy.start()

    def far_backward_q(h, carry):
        k_t, v_t = all_cols(0, h), all_cols(1, h)
        d = fr_s[h]
        term = d[DH:DH + 1]
        term_hi = term.astype(BF16).astype(F32)
        left = jnp.concatenate([d[:DH], term_hi, term - term_hi, jnp.zeros((62, SUB), F32)], 0).T.astype(BF16)
        ones = jnp.concatenate([jnp.ones((2, SPAN), BF16), jnp.zeros((62, SPAN), BF16)], 0)
        dprob = nn(left, jnp.concatenate([v_t, ones], 0))
        dscore = dprob.astype(BF16) * fe_s[h]
        fq_s[h] = nt(dscore, k_t).T * SCALE
        return carry

    for h in range(HEADS):
        far_backward_q(h, 0)
    fq_copy = pltpu.make_async_copy(fq_s, fq_hbm, own_sem.at[5])
    fq_copy.start()

    quarter, wide = half // 2, D // 2
    b_out, b_in = [], []
    for k in range(1, 4):
        b_out.append(pltpu.make_async_remote_copy(
            b_send.at[(x + k) % 4], b_recv.at[x], b_ss.at[k - 1], b_rs.at[k - 1],
            device_id=same_core[k - 1], device_id_type=MESH))
        b_in.append(pltpu.make_async_remote_copy(
            b_send.at[(x + k) % 4], b_recv.at[(x + 4 - k) % 4], b_ss.at[k - 1], b_rs.at[k - 1],
            device_id=same_core[k - 1], device_id_type=MESH))
    c_out, c_in = [], []
    for k in range(1, 4):
        c_out.append(pltpu.make_async_remote_copy(
            c_buf.at[yg], c_buf.at[yg], c_ss.at[k - 1], c_rs.at[k - 1], device_id=y_peers[k - 1], device_id_type=MESH))
        there = (yg + 4 - k) % 4
        c_in.append(pltpu.make_async_remote_copy(
            c_buf.at[there], c_buf.at[there], c_ss.at[k - 1], c_rs.at[k - 1], device_id=y_peers[k - 1], device_id_type=MESH))
    d_out, d_in = [], []
    d_peers = [same_core[k - 1] for k in range(1, 4)] + [sibling] + other_core
    for k in range(1, 8):
        d_out.append(pltpu.make_async_remote_copy(
            d_own, d_far.at[core, x], d_ss.at[k - 1], d_rs.at[k - 1], device_id=d_peers[k - 1], device_id_type=MESH))
        theirs = d_far.at[core if k < 4 else 1 - core, (x + 4 - k % 4) % 4]
        d_in.append(pltpu.make_async_remote_copy(
            d_own, theirs, d_ss.at[k - 1], d_rs.at[k - 1], device_id=d_peers[k - 1], device_id_type=MESH))
    d_copy = pltpu.make_async_copy(d_own, d_far.at[core, x], own_sem.at[6])

    def outs(h):
        return [
            pltpu.make_async_copy(aq_s.at[h], aq_hbm.at[h], out_sem.at[0, h]),
            pltpu.make_async_copy(ak_s.at[h], ak_hbm.at[h], out_sem.at[1, h]),
            pltpu.make_async_copy(av_s.at[h], av_hbm.at[h], out_sem.at[2, h]),
        ]


    def near_backward(u, carry):
        h, off = u // 2, pl.multiple_of((u % 2) * SEG, SEG)
        rows = pl.ds(off, SEG)
        q_t, k_t, v_t, gh = q_s[h, :, rows], k_s[h, :, rows], v_s[h, :, rows], nd_s[h, :, rows]
        th, tl = hi_lo(st_s[h, 2:3, rows])
        gg = jnp.concatenate([gh, jnp.concatenate([th, tl, jnp.zeros((14, SEG), BF16)], 0)], 0)
        vv = jnp.concatenate([v_t, jnp.ones((2, SEG), BF16), jnp.zeros((14, SEG), BF16)], 0).T
        for ib in range(2):
            cols = slice(ib * 512, ib * 512 + 512)
            dprob = nn(vv, gg[:, cols])
            ds = dprob.astype(BF16) * e_s[u, :, cols]
            ds_s[:, cols] = ds
            aq_s[h, :, pl.ds(pl.multiple_of(off + ib * 512, 512), 512)] = (nn(k_t, ds) * SCALE).astype(BF16)
        for jb in range(2):
            cols = slice(jb * 512, jb * 512 + 512)
            out_cols = pl.ds(pl.multiple_of(off + jb * 512, 512), 512)
            ak_s[h, :, out_cols] = (nt(ds_s[cols, :], q_t).T * SCALE).astype(BF16)
            av_s[h, :, out_cols] = nt(e_s[u, cols, :], gh).T.astype(BF16)

        @pl.when(u % 2 == 1)
        def _():
            for c in outs(h):
                c.start()

        @pl.when(u == 0)
        def _():
            for c in own_copies:
                c.wait()
            for c in q_in:
                c.wait_recv()
            q_pair[0].start()
            a_copy.wait()
            mine = gw_s[pl.ds(pl.multiple_of(core * half, 32), half), :]
            half_s[...] = mine + a_recv[...].astype(F32)
            for t in range(4):
                b_send[t] = half_s[(t // 2) * quarter:(t // 2 + 1) * quarter, (t % 2) * wide:(t % 2 + 1) * wide].astype(BF16)
            for c in b_out + do_out[14:]:
                c.start()

        @pl.when(u == 1)
        def _():
            for c in b_in:
                c.wait_recv()
            b_recv[x] = b_send[x]
            total = b_recv[0].astype(F32)
            for t in range(1, 4):
                total = total + b_recv[t].astype(F32)
            c_buf[yg] = total.astype(BF16)
            for c in c_out:
                c.start()

        @pl.when(u == 3)
        def _():
            for c in c_in:
                c.wait_recv()
            total = c_buf[0].astype(F32)
            for t in range(1, 4):
                total = total + c_buf[t].astype(F32)
            d_own[...] = total.astype(BF16)
            for c in d_out:
                c.start()
            d_copy.start()

        @pl.when(u == 4)
        def _():
            for c in do_in:
                c.wait_recv()
            do_copy.wait()
            do_pair[0].start()

        return carry

    lax.fori_loop(0, 2 * HEADS, near_backward, 0)
    fq_copy.wait()
    d_copy.wait()
    for sends in kv_out:
        for c in sends:
            c.wait_send()
    for pair in kv_pair + [q_pair, do_pair]:
        pair[0].wait_send()
    for c in q_out + do_out + b_out + c_out + d_out:
        c.wait_send()
    q_pair[1].wait_recv()
    do_pair[1].wait_recv()
    for c in d_in:
        c.wait_recv()
    for h in range(HEADS):
        for c in outs(h):
            c.wait()


def back_kernel(
    phases, valid, aq_hbm, ak_hbm, av_hbm, fq_hbm, own_hbm, q_far, do_far, d_far,
    dq_hbm, dk_hbm, dv_hbm, gw_hbm,
    aq_s, ak_s, av_s, fq_s, own_s, q_buf, do_buf, d_buf, oq_s, ok_s, ov_s, gw_s, in_sem, out_sem,
):
    sq = lax.axis_index("seq")
    pairs = ((q_far, q_buf), (own_hbm, own_s), (do_far, do_buf), (fq_hbm, fq_s),
             (aq_hbm, aq_s), (ak_hbm, ak_s), (av_hbm, av_s), (d_far, d_buf))
    copies = [pltpu.make_async_copy(a, b, in_sem.at[n]) for n, (a, b) in enumerate(pairs)]
    for c in copies:
        c.start()

    def all_cols(buf, h, lo, hi):
        return jnp.concatenate([buf[n % 2, n // 2, h, lo:hi, :] for n in range(PEERS)], 1)

    def far_backward_kv(h):
        ph = phases[h]
        q_t, do_t = all_cols(q_buf, h, 0, DH), all_cols(do_buf, h, 0, DH)
        stats = all_cols(do_buf, h, DH, DO_ROWS)
        own_k = own_s[0, h].astype(F32) * (SCALE * LOG2E)
        own_v = own_s[1, h].astype(F32)
        hi = own_k.astype(BF16).astype(F32)
        index = lax.broadcasted_iota(jnp.int32, (16, SUB), 0)
        first = jnp.where(index < 3, 1.0, 0.0)
        second = jnp.where((index >= 3) & (index < 6), 1.0, 0.0)
        zeros = jnp.zeros((48, SUB), F32)
        left_s = jnp.concatenate([hi, own_k - hi, first, zeros, zeros, jnp.zeros((16, SUB), F32)], 0).T.astype(BF16)
        s = nn(left_s[:, :QD_ROWS], jnp.concatenate([q_t, q_t, stats], 0))
        j = lax.broadcasted_iota(jnp.int32, (SUB, 1), 0)
        row = sq * ROWS + (j >> 5) * (RATE * BLK) + ph * BLK + (j & 31)
        probs = jnp.where(row < valid[0], jnp.exp2(s), 0.0).astype(BF16)
        left_d = jnp.concatenate([own_v, second, zeros], 0).T.astype(BF16)
        dprob = nn(left_d[:, :DH + 16], jnp.concatenate([do_t, stats], 0))
        dscore = dprob.astype(BF16) * probs
        return jnp.concatenate([nt(dscore, q_t) * SCALE, nt(probs, do_t)], 1).T

    outs = []

    def finish(n, near, far, out, dest):
        for h in range(HEADS):
            parts = place_parts(far[h], phases[h])
            for c in range(16):
                cols = pl.ds(c * 128, 128)
                placed = jnp.where(place_mask(phases[h], c), parts[c // 4], 0.0)
                out[h, :, cols] = (near[h, :, cols].astype(F32) + placed).astype(BF16)
        outs.append(pltpu.make_async_copy(out, dest.at[0], out_sem.at[n]))
        outs[-1].start()

    for c in copies[:5]:
        c.wait()
    finish(0, aq_s, fq_s, oq_s, dq_hbm)
    both = [far_backward_kv(h) for h in range(HEADS)]
    for c in copies[5:]:
        c.wait()
    finish(1, ak_s, [b[:DH] for b in both], ok_s, dk_hbm)
    half, quarter, wide = HEADS * DH // 2, HEADS * DH // 4, D // 2
    for cc in range(2):
        for t in range(4):
            gw_s[cc * half + (t // 2) * quarter:cc * half + (t // 2 + 1) * quarter, (t % 2) * wide:(t % 2 + 1) * wide] = (
                d_buf[cc, t].astype(F32))
    outs.append(pltpu.make_async_copy(gw_s, gw_hbm, out_sem.at[3]))
    outs[-1].start()
    finish(2, av_s, [b[DH:] for b in both], ov_s, dv_hbm)
    for c in outs:
        c.wait()


def shards(queries, key_states, value_states, out_weight, grad_output, phases, valid_rows):
    big = lambda dtype: pltpu.VMEM((HEADS, DH, ROWS), dtype)
    dma = pltpu.SemaphoreType.DMA
    any_spec = pl.BlockSpec(memory_space=pl.ANY)
    smem = pl.BlockSpec(memory_space=pltpu.SMEM)
    chunk = (HEADS * DH // 4, D // 2)
    state = jax.ShapeDtypeStruct(queries.shape, BF16)
    near = jax.ShapeDtypeStruct((HEADS, DH, ROWS), BF16)
    shape = jax.ShapeDtypeStruct
    passed = [
        near, near, near, shape((HEADS, DH, SUB), F32), shape((2, HEADS, DH, SUB), BF16),
        shape((2, 8, HEADS, DH, SUB), BF16), shape((2, 8, HEADS, DO_ROWS, SUB), BF16), shape((2, 4, *chunk), BF16)]
    between = pl.pallas_call(
        front_kernel,
        out_shape=passed,
        in_specs=[smem, smem] + [any_spec] * 5,
        out_specs=[any_spec] * 8,
        scratch_shapes=[
            big(BF16), big(BF16), big(BF16),
            pltpu.VMEM((HEADS * DH, D), BF16), pltpu.VMEM((ROWS, D), BF16),
            big(BF16),
            pltpu.VMEM((2 * HEADS, SEG, SEG), BF16), pltpu.VMEM((SEG, SEG), BF16),
            big(F32), pltpu.VMEM((HEADS, 8, ROWS), F32), big(BF16), big(BF16),
            pltpu.VMEM((2, 2, 8, HEADS, DH, SUB), BF16),
            pltpu.VMEM((HEADS, DH, SUB), BF16), pltpu.VMEM((HEADS, DO_ROWS, SUB), BF16),
            pltpu.VMEM((HEADS, SUB, D), BF16),
            pltpu.VMEM((HEADS, SUB, SPAN), BF16), pltpu.VMEM((HEADS, DH, SUB), F32), pltpu.VMEM((HEADS, DH + 8, SUB), F32),
            big(BF16), big(BF16), big(BF16),
            pltpu.VMEM((HEADS * DH, D), F32),
            pltpu.VMEM((HEADS * DH // 2, D), BF16), pltpu.VMEM((HEADS * DH // 2, D), BF16),
            pltpu.VMEM((HEADS * DH // 2, D), F32),
            pltpu.VMEM((4, *chunk), BF16), pltpu.VMEM((4, *chunk), BF16), pltpu.VMEM((4, *chunk), BF16),
            pltpu.VMEM(chunk, BF16),
            dma((5,)), dma((3, HEADS)), dma((7,)), dma((21,)), dma((21,)), dma((28,)), dma((28,)), dma((5,)), dma((5,)),
            dma((2,)), dma((3,)), dma((3,)), dma((3,)), dma((3,)), dma((7,)), dma((7,)),
        ],
        compiler_params=pltpu.CompilerParams(
            collective_id=0, has_side_effects=True, vmem_limit_bytes=58 << 20),
        name="front",
    )(phases, valid_rows, queries, key_states, value_states, out_weight, grad_output)
    return pl.pallas_call(
        back_kernel,
        out_shape=[state, state, state, shape((HEADS * DH, D), F32)],
        in_specs=[smem, smem] + [any_spec] * 8,
        out_specs=[any_spec] * 4,
        scratch_shapes=[pltpu.VMEM(p.shape, p.dtype) for p in passed] + [
            big(BF16), big(BF16), big(BF16), pltpu.VMEM((HEADS * DH, D), F32), dma((8,)), dma((4,))],
        compiler_params=pltpu.CompilerParams(vmem_limit_bytes=58 << 20),
        name="back",
    )(phases, valid_rows, *between)


def solution(mesh):
    heads = P("dp", "tensor", None, "seq")
    return jax.shard_map(
        shards, mesh=mesh,
        in_specs=(heads, heads, heads, P("tensor", None), P("dp", "seq", None), P("tensor"), P("dp")),
        out_specs=(heads, heads, heads, P("tensor", None)),
        check_vma=False,
    )
```

```python
import jax
import jax.numpy as jnp
from jax import lax
from jax.experimental import pallas as pl
from jax.experimental.pallas import tpu as pltpu
from jax.sharding import PartitionSpec as P

F32 = jnp.float32
BF16 = jnp.bfloat16
SEG = 1024
RATE = 16
BLK = 32
HEADS = 3
DH = 64
ROWS = 2048
SUB = ROWS // RATE
D = 768
PEERS = 16
SPAN = PEERS * SUB
SCALE = 0.125
LOG2E = 1.4426950408889634
DO_ROWS = 80
QD_ROWS = DH + DO_ROWS
MESH = pl.DeviceIdType.MESH


def nn(a, b):
    return jnp.dot(a, b, preferred_element_type=F32)


def nt(a, b):
    return lax.dot_general(a, b, (((1,), (1,)), ((), ())), preferred_element_type=F32)


def hi_lo(x):
    hi = x.astype(BF16)
    return hi, (x - hi.astype(F32)).astype(BF16)


def split3(x):
    hi = x.astype(BF16)
    rest = x - hi.astype(F32)
    mid = rest.astype(BF16)
    return hi, mid, (rest - mid.astype(F32)).astype(BF16)


def lanes(n=SUB):
    return lax.broadcasted_iota(jnp.int32, (1, n), 1)


def turn(x, groups):
    groups = groups % 4
    return x if groups == 0 else pltpu.roll(x, groups * 32, 1)


def choose(options, which):
    out = options[0]
    for n in range(1, len(options)):
        out = jnp.where(which == n, options[n], out)
    return out


def pick(load, phase):
    chunk = jnp.full((1, SUB), phase >> 2, jnp.int32)
    part = jnp.full((1, SUB), phase & 3, jnp.int32)
    group = lanes() >> 5
    out = None
    for b in range(4):
        x = choose([load(b * 512 + n * 128).astype(F32) for n in range(4)], chunk)
        x = choose([turn(x, b - n) for n in range(4)], part)
        out = x if b == 0 else jnp.where(group == b, x, out)
    return out


def place_parts(x, phase):
    part = jnp.full((1, SUB), phase & 3, jnp.int32)
    turned = [turn(x, n) for n in range(4)]
    return [choose([turned[(n - b) % 4] for n in range(4)], part) for b in range(4)]


def place_mask(phase, c):
    want = jnp.where((phase >> 2) == (c % 4), phase & 3, -1)
    return (lanes() >> 5) == want


def front_kernel(
    phases, valid, q_hbm, k_hbm, v_hbm, w_hbm, go_hbm,
    aq_hbm, ak_hbm, av_hbm, fq_hbm, own_hbm, q_far, do_far, d_far,
    q_s, k_s, v_s, w_s, go_s, g_s, e_s, ds_s, on_s, st_s, nd_s, at_s,
    kv_buf, q_own, do_own, gp_s, fe_s, fq_s, fr_s, aq_s, ak_s, av_s,
    gw_s, a_send, a_recv, half_s, b_send, b_recv, c_buf, d_own,
    in_sem, out_sem, own_sem, kv_send, kv_recv, qd_send, qd_recv, pair_send, pair_recv,
    a_sem, b_ss, b_rs, c_ss, c_rs, d_ss, d_rs,
):
    dp, sq, tz = lax.axis_index("dp"), lax.axis_index("seq"), lax.axis_index("tensor")
    y, x, core = sq // 8, (sq % 8) // 2, sq % 2
    yx = sq // 2
    yg = dp * 2 + y

    copies = [
        pltpu.make_async_copy(k_hbm.at[0], k_s, in_sem.at[0]),
        pltpu.make_async_copy(v_hbm.at[0], v_s, in_sem.at[1]),
        pltpu.make_async_copy(q_hbm.at[0], q_s, in_sem.at[2]),
        pltpu.make_async_copy(w_hbm, w_s, in_sem.at[3]),
        pltpu.make_async_copy(go_hbm.at[0], go_s, in_sem.at[4]),
    ]
    for c in copies:
        c.start()

    def at_yx(k):
        yy, xx = (y + k // 4) % 2, (x + k % 4) % 4
        return yy * 4 + xx

    def from_yx(k):
        yy, xx = (y + 2 - k // 4) % 2, (x + 4 - k % 4) % 4
        return yy * 4 + xx

    same_core = [(dp, at_yx(k) * 2 + core, tz) for k in range(1, 8)]
    sibling = (dp, yx * 2 + 1 - core, tz)
    other_core = [(dp, (y * 4 + (x + k) % 4) * 2 + 1 - core, tz) for k in range(1, 4)]
    y_peers = []
    for k in range(1, 4):
        there = (yg + k) % 4
        y_peers.append((there // 2, (there % 2) * 8 + x * 2 + core, tz))
    barrier = pltpu.get_barrier_semaphore()
    dp_peers = [(1 - dp, yy * 8 + x * 2 + core, tz) for yy in range(2)]
    greet = same_core + [sibling] + other_core + dp_peers
    for peer in greet:
        pl.semaphore_signal(barrier, inc=1, device_id=peer, device_id_type=MESH)

    def pick_into(t, ref):
        copies[t].wait()
        for h in range(HEADS):
            kv_buf[core, t, yx, h] = pick(lambda o: ref[h, :, pl.ds(o, 128)], phases[h]).astype(BF16)

    pick_into(0, k_s)
    pl.semaphore_wait(barrier, len(greet))

    def gather(mine, slot, ss, rs, base):
        sends, recvs = [], []
        for k in (6, 5, 7, 2, 4, 1, 3):
            n = base + k - 1
            sends.append(pltpu.make_async_remote_copy(
                mine, slot(yx), ss.at[n], rs.at[n], device_id=same_core[k - 1], device_id_type=MESH))
            recvs.append(pltpu.make_async_remote_copy(
                mine, slot(from_yx(k)), ss.at[n], rs.at[n], device_id=same_core[k - 1], device_id_type=MESH))
        return sends, recvs

    def to_pair(buf, i):
        out = pltpu.make_async_remote_copy(
            buf(core), buf(core), pair_send.at[i], pair_recv.at[i], device_id=sibling, device_id_type=MESH)
        back = pltpu.make_async_remote_copy(
            buf(1 - core), buf(1 - core), pair_send.at[i], pair_recv.at[i], device_id=sibling, device_id_type=MESH)
        return out, back

    kv_out, kv_in, kv_pair = [], [], []
    for t in range(2):
        if t == 1:
            pick_into(1, v_s)
        sends, recvs = gather(kv_buf.at[core, t, yx], lambda n, t=t: kv_buf.at[core, t, n], kv_send, kv_recv, 7 * t)
        kv_out.append(sends)
        kv_in.append(recvs)
        kv_pair.append(to_pair(lambda c, t=t: kv_buf.at[c, t], t))
        for c in sends:
            c.start()

    copies[2].wait()
    for h in range(HEADS):
        q_own[h] = pick(lambda o: q_s[h, :, pl.ds(o, 128)], phases[h]).astype(BF16)
    own_copies = [
        pltpu.make_async_copy(kv_buf.at[core, t, yx], own_hbm.at[t], own_sem.at[t]) for t in range(2)]
    own_copies.append(pltpu.make_async_copy(q_own, q_far.at[core, yx], own_sem.at[3]))
    for c in own_copies:
        c.start()

    def forward_pair(h):
        for c in kv_in[h]:
            c.wait_recv()
        kv_pair[h][0].start()

    def near_forward(u, carry):
        h, off = u // 2, pl.multiple_of((u % 2) * SEG, SEG)
        rows = pl.ds(off, SEG)
        k_t, v_t = k_s[h, :, rows], v_s[h, :, rows]
        qh, ql = hi_lo(q_s[h, :, rows].astype(F32) * (SCALE * LOG2E))
        kk = jnp.concatenate([k_t, k_t], 0).T
        s = nn(kk, jnp.concatenate([qh, ql], 0))
        m = jnp.max(s, axis=0, keepdims=True)
        e = jnp.exp2(s - m).astype(BF16)
        e_s[u] = e
        o = nn(jnp.concatenate([v_t, jnp.ones((16, SEG), BF16)], 0), e)
        total = o[DH:DH + 1]
        r = 1.0 / total
        on_s[h, :, rows] = o[:DH] * r
        st_s[h, 0:1, rows] = r
        st_s[h, 1:2, rows] = m + jnp.log2(total)
        return carry

    for u in range(2 * HEADS):
        near_forward(u, 0)
    forward_pair(0)
    copies[3].wait()
    copies[4].wait()
    g_s[...] = nt(w_s[...], go_s[...]).astype(BF16).reshape(HEADS, DH, ROWS)
    for h in range(HEADS):
        for c in range(16):
            cols = pl.ds(c * 128, 128)
            near = on_s[h, :, cols]
            rr = st_s[h, 0:1, cols]
            nd = (g_s[h, :, cols].astype(F32) * rr).astype(BF16)
            nd_s[h, :, cols] = nd
            st_s[h, 2:3, cols] = -jnp.sum(nd.astype(F32) * near, axis=0, keepdims=True)
            at_s[h, :, cols] = jnp.where(place_mask(phases[h], c), 0.0, near).astype(BF16)
    forward_pair(1)
    gw_s[...] = nn(at_s[...].reshape(HEADS * DH, ROWS), go_s[...])
    q_out, q_in = gather(q_own, lambda n: q_far.at[core, n], qd_send, qd_recv, 0)
    q_pair = to_pair(lambda c: q_far.at[c], HEADS)
    for c in q_out:
        c.start()

    for h in range(HEADS):
        which = jnp.full((1, D), phases[h], jnp.int32)
        for b in range(4):
            rows = [go_s[b * 512 + n * BLK:b * 512 + (n + 1) * BLK, :] for n in range(RATE)]
            gp_s[h, b * BLK:(b + 1) * BLK, :] = choose(rows, which)

    key_index = lanes(SPAN)

    def all_cols(t, h):
        return jnp.concatenate([kv_buf[n % 2, t, n // 2, h] for n in range(PEERS)], 1)

    def far_scores(h):
        ph = phases[h]
        k_t = all_cols(0, h)
        q_t = q_own[h].astype(F32) * (SCALE * LOG2E)
        hi = q_t.astype(BF16).astype(F32)
        lhs = jnp.concatenate([hi, q_t - hi], 0).T.astype(BF16)
        s = nn(lhs, jnp.concatenate([k_t, k_t], 0))
        row = (key_index >> 5) * (RATE * BLK) + ph * BLK + (key_index & 31)
        s = jnp.where(row < valid[0], s, -1e30)
        m = jnp.max(s, axis=1, keepdims=True)
        e = jnp.exp2(s - m).astype(BF16)
        fe_s[h] = e
        return m

    def far_forward(h, m):
        ph = phases[h]
        e, v_t = fe_s[h], all_cols(1, h)
        o = nt(e, jnp.concatenate([v_t, jnp.ones((16, SPAN), BF16)], 0))
        total = o[:, DH:DH + 1]
        r = 1.0 / total
        packed = jnp.concatenate(
            [o[:, :DH] * r, jnp.broadcast_to(m + jnp.log2(total), (SUB, 32)), jnp.broadcast_to(r, (SUB, 32))], 1).T
        far_out, far_lse, far_r = packed[0:DH], packed[DH:DH + 1], packed[96:97]
        near_out = pick(lambda o: on_s[h, :, pl.ds(o, 128)], ph)
        near_stats = pick(lambda o: st_s[h, :, pl.ds(o, 128)], ph)
        near_r, near_lse = near_stats[0:1], near_stats[1:2]
        g = pick(lambda o: g_s[h, :, pl.ds(o, 128)], ph)
        mixing = 1.0 / (1.0 + jnp.exp2(near_lse - far_lse))
        rest = 1.0 / (1.0 + jnp.exp2(far_lse - near_lse))
        diff = far_out - near_out
        comb = near_out + mixing * diff
        far_dlse = jnp.sum(g * diff, axis=0, keepdims=True) * mixing * rest
        far_dout = (mixing * g).astype(BF16)
        fd = far_dout.astype(F32)
        term = far_dlse - jnp.sum(fd * far_out, axis=0, keepdims=True)
        do_own[h, 0:DH, :] = far_dout
        do_own[h, DH:DO_ROWS, :] = jnp.concatenate(
            [*split3(-far_lse), *split3(term), jnp.zeros((10, SUB), BF16)], 0)
        scaled = (fd * far_r).astype(BF16).astype(F32)
        term_r = far_dlse * far_r - jnp.sum(scaled * far_out, axis=0, keepdims=True)
        fr_s[h, 0:DH, :] = scaled
        fr_s[h, DH:DH + 8, :] = jnp.broadcast_to(term_r, (8, SUB))
        gw_s[h * DH:(h + 1) * DH, :] += nn(comb.astype(BF16), gp_s[h])
        near_dout = (rest * g).astype(BF16).astype(F32)
        nd = (near_dout * near_r).astype(BF16).astype(F32)
        near_term = -far_dlse * near_r - jnp.sum(nd * near_out, axis=0, keepdims=True)
        parts = place_parts(jnp.concatenate([nd, near_term, jnp.zeros((7, SUB), F32)], 0), ph)
        for c in range(16):
            cols = pl.ds(c * 128, 128)
            mask = place_mask(ph, c)
            part = parts[c // 4]
            nd_s[h, :, cols] = jnp.where(mask, part[:DH], nd_s[h, :, cols].astype(F32)).astype(BF16)
            st_s[h, 2:3, cols] = jnp.where(mask, part[DH:DH + 1], st_s[h, 2:3, cols])

    kv_pair[0][1].wait_recv()
    tops = [far_scores(h) for h in range(HEADS)]
    kv_pair[1][1].wait_recv()
    for h in range(HEADS):
        far_forward(h, tops[h])

    do_out, do_in = [], []
    for h in range(HEADS):
        sends, recvs = gather(do_own.at[h], lambda n, h=h: do_far.at[core, n, h], qd_send, qd_recv, 7 + 7 * h)
        do_out += sends
        do_in += recvs
    do_pair = to_pair(lambda c: do_far.at[c], HEADS + 1)
    for c in do_out[:14]:
        c.start()
    do_copy = pltpu.make_async_copy(do_own, do_far.at[core, yx], own_sem.at[4])
    do_copy.start()

    half = HEADS * DH // 2
    a_send[...] = gw_s[pl.ds(pl.multiple_of((1 - core) * half, 32), half), :].astype(BF16)
    a_copy = pltpu.make_async_remote_copy(a_send, a_recv, a_sem.at[0], a_sem.at[1], device_id=sibling, device_id_type=MESH)
    a_copy.start()

    def far_backward_q(h, carry):
        k_t, v_t = all_cols(0, h), all_cols(1, h)
        d = fr_s[h]
        term = d[DH:DH + 1]
        term_hi = term.astype(BF16).astype(F32)
        left = jnp.concatenate([d[:DH], term_hi, term - term_hi, jnp.zeros((62, SUB), F32)], 0).T.astype(BF16)
        ones = jnp.concatenate([jnp.ones((2, SPAN), BF16), jnp.zeros((62, SPAN), BF16)], 0)
        dprob = nn(left, jnp.concatenate([v_t, ones], 0))
        dscore = dprob.astype(BF16) * fe_s[h]
        fq_s[h] = nt(dscore, k_t).T * SCALE
        return carry

    for h in range(HEADS):
        far_backward_q(h, 0)
    fq_copy = pltpu.make_async_copy(fq_s, fq_hbm, own_sem.at[5])
    fq_copy.start()

    quarter, wide = half // 2, D // 2
    b_out, b_in = [], []
    for k in range(1, 4):
        b_out.append(pltpu.make_async_remote_copy(
            b_send.at[(x + k) % 4], b_recv.at[x], b_ss.at[k - 1], b_rs.at[k - 1],
            device_id=same_core[k - 1], device_id_type=MESH))
        b_in.append(pltpu.make_async_remote_copy(
            b_send.at[(x + k) % 4], b_recv.at[(x + 4 - k) % 4], b_ss.at[k - 1], b_rs.at[k - 1],
            device_id=same_core[k - 1], device_id_type=MESH))
    c_out, c_in = [], []
    for k in range(1, 4):
        c_out.append(pltpu.make_async_remote_copy(
            c_buf.at[yg], c_buf.at[yg], c_ss.at[k - 1], c_rs.at[k - 1], device_id=y_peers[k - 1], device_id_type=MESH))
        there = (yg + 4 - k) % 4
        c_in.append(pltpu.make_async_remote_copy(
            c_buf.at[there], c_buf.at[there], c_ss.at[k - 1], c_rs.at[k - 1], device_id=y_peers[k - 1], device_id_type=MESH))
    d_out, d_in = [], []
    d_peers = [same_core[k - 1] for k in range(1, 4)] + [sibling] + other_core
    for k in range(1, 8):
        d_out.append(pltpu.make_async_remote_copy(
            d_own, d_far.at[core, x], d_ss.at[k - 1], d_rs.at[k - 1], device_id=d_peers[k - 1], device_id_type=MESH))
        theirs = d_far.at[core if k < 4 else 1 - core, (x + 4 - k % 4) % 4]
        d_in.append(pltpu.make_async_remote_copy(
            d_own, theirs, d_ss.at[k - 1], d_rs.at[k - 1], device_id=d_peers[k - 1], device_id_type=MESH))
    d_copy = pltpu.make_async_copy(d_own, d_far.at[core, x], own_sem.at[6])

    def outs(h):
        return [
            pltpu.make_async_copy(aq_s.at[h], aq_hbm.at[h], out_sem.at[0, h]),
            pltpu.make_async_copy(ak_s.at[h], ak_hbm.at[h], out_sem.at[1, h]),
            pltpu.make_async_copy(av_s.at[h], av_hbm.at[h], out_sem.at[2, h]),
        ]


    def near_backward(u, carry):
        h, off = u // 2, pl.multiple_of((u % 2) * SEG, SEG)
        rows = pl.ds(off, SEG)
        q_t, k_t, v_t, gh = q_s[h, :, rows], k_s[h, :, rows], v_s[h, :, rows], nd_s[h, :, rows]
        th, tl = hi_lo(st_s[h, 2:3, rows])
        gg = jnp.concatenate([gh, jnp.concatenate([th, tl, jnp.zeros((14, SEG), BF16)], 0)], 0)
        vv = jnp.concatenate([v_t, jnp.ones((2, SEG), BF16), jnp.zeros((14, SEG), BF16)], 0).T
        for ib in range(2):
            cols = slice(ib * 512, ib * 512 + 512)
            dprob = nn(vv, gg[:, cols])
            ds = dprob.astype(BF16) * e_s[u, :, cols]
            ds_s[:, cols] = ds
            aq_s[h, :, pl.ds(pl.multiple_of(off + ib * 512, 512), 512)] = (nn(k_t, ds) * SCALE).astype(BF16)
        for jb in range(2):
            cols = slice(jb * 512, jb * 512 + 512)
            out_cols = pl.ds(pl.multiple_of(off + jb * 512, 512), 512)
            ak_s[h, :, out_cols] = (nt(ds_s[cols, :], q_t).T * SCALE).astype(BF16)
            av_s[h, :, out_cols] = nt(e_s[u, cols, :], gh).T.astype(BF16)

        @pl.when(u % 2 == 1)
        def _():
            for c in outs(h):
                c.start()

        @pl.when(u == 0)
        def _():
            for c in own_copies:
                c.wait()
            for c in q_in:
                c.wait_recv()
            q_pair[0].start()
            a_copy.wait()
            mine = gw_s[pl.ds(pl.multiple_of(core * half, 32), half), :]
            half_s[...] = mine + a_recv[...].astype(F32)
            for t in range(4):
                b_send[t] = half_s[(t // 2) * quarter:(t // 2 + 1) * quarter, (t % 2) * wide:(t % 2 + 1) * wide].astype(BF16)
            for c in b_out + do_out[14:]:
                c.start()

        @pl.when(u == 1)
        def _():
            for c in b_in:
                c.wait_recv()
            b_recv[x] = b_send[x]
            total = b_recv[0].astype(F32)
            for t in range(1, 4):
                total = total + b_recv[t].astype(F32)
            c_buf[yg] = total.astype(BF16)
            for c in c_out:
                c.start()

        @pl.when(u == 3)
        def _():
            for c in c_in:
                c.wait_recv()
            total = c_buf[0].astype(F32)
            for t in range(1, 4):
                total = total + c_buf[t].astype(F32)
            d_own[...] = total.astype(BF16)
            for c in d_out:
                c.start()
            d_copy.start()

        @pl.when(u == 4)
        def _():
            for c in do_in:
                c.wait_recv()
            do_copy.wait()
            do_pair[0].start()

        return carry

    lax.fori_loop(0, 2 * HEADS, near_backward, 0)
    fq_copy.wait()
    d_copy.wait()
    for sends in kv_out:
        for c in sends:
            c.wait_send()
    for pair in kv_pair + [q_pair, do_pair]:
        pair[0].wait_send()
    for c in q_out + do_out + b_out + c_out + d_out:
        c.wait_send()
    q_pair[1].wait_recv()
    do_pair[1].wait_recv()
    for c in d_in:
        c.wait_recv()
    for h in range(HEADS):
        for c in outs(h):
            c.wait()


def back_kernel(
    phases, valid, aq_hbm, ak_hbm, av_hbm, fq_hbm, own_hbm, q_far, do_far, d_far,
    dq_hbm, dk_hbm, dv_hbm, gw_hbm,
    aq_s, ak_s, av_s, fq_s, own_s, q_buf, do_buf, d_buf, oq_s, ok_s, ov_s, gw_s, in_sem, out_sem,
):
    sq = lax.axis_index("seq")
    pairs = ((q_far, q_buf), (own_hbm, own_s), (do_far, do_buf), (fq_hbm, fq_s),
             (aq_hbm, aq_s), (ak_hbm, ak_s), (av_hbm, av_s), (d_far, d_buf))
    copies = [pltpu.make_async_copy(a, b, in_sem.at[n]) for n, (a, b) in enumerate(pairs)]
    for c in copies:
        c.start()

    def all_cols(buf, h, lo, hi):
        return jnp.concatenate([buf[n % 2, n // 2, h, lo:hi, :] for n in range(PEERS)], 1)

    def far_backward_kv(h):
        ph = phases[h]
        q_t, do_t = all_cols(q_buf, h, 0, DH), all_cols(do_buf, h, 0, DH)
        stats = all_cols(do_buf, h, DH, DO_ROWS)
        own_k = own_s[0, h].astype(F32) * (SCALE * LOG2E)
        own_v = own_s[1, h].astype(F32)
        hi = own_k.astype(BF16).astype(F32)
        index = lax.broadcasted_iota(jnp.int32, (16, SUB), 0)
        first = jnp.where(index < 3, 1.0, 0.0)
        second = jnp.where((index >= 3) & (index < 6), 1.0, 0.0)
        zeros = jnp.zeros((48, SUB), F32)
        left_s = jnp.concatenate([hi, own_k - hi, first, zeros, zeros, jnp.zeros((16, SUB), F32)], 0).T.astype(BF16)
        s = nn(left_s[:, :QD_ROWS], jnp.concatenate([q_t, q_t, stats], 0))
        j = lax.broadcasted_iota(jnp.int32, (SUB, 1), 0)
        row = sq * ROWS + (j >> 5) * (RATE * BLK) + ph * BLK + (j & 31)
        probs = jnp.where(row < valid[0], jnp.exp2(s), 0.0).astype(BF16)
        left_d = jnp.concatenate([own_v, second, zeros], 0).T.astype(BF16)
        dprob = nn(left_d[:, :DH + 16], jnp.concatenate([do_t, stats], 0))
        dscore = dprob.astype(BF16) * probs
        return jnp.concatenate([nt(dscore, q_t) * SCALE, nt(probs, do_t)], 1).T

    outs = []

    def finish(n, near, far, out, dest):
        for h in range(HEADS):
            parts = place_parts(far[h], phases[h])
            for c in range(16):
                cols = pl.ds(c * 128, 128)
                placed = jnp.where(place_mask(phases[h], c), parts[c // 4], 0.0)
                out[h, :, cols] = (near[h, :, cols].astype(F32) + placed).astype(BF16)
        outs.append(pltpu.make_async_copy(out, dest.at[0], out_sem.at[n]))
        outs[-1].start()

    for c in copies[:5]:
        c.wait()
    finish(0, aq_s, fq_s, oq_s, dq_hbm)
    both = [far_backward_kv(h) for h in range(HEADS)]
    for c in copies[5:]:
        c.wait()
    finish(1, ak_s, [b[:DH] for b in both], ok_s, dk_hbm)
    half, quarter, wide = HEADS * DH // 2, HEADS * DH // 4, D // 2
    for cc in range(2):
        for t in range(4):
            gw_s[cc * half + (t // 2) * quarter:cc * half + (t // 2 + 1) * quarter, (t % 2) * wide:(t % 2 + 1) * wide] = (
                d_buf[cc, t].astype(F32))
    outs.append(pltpu.make_async_copy(gw_s, gw_hbm, out_sem.at[3]))
    outs[-1].start()
    finish(2, av_s, [b[DH:] for b in both], ov_s, dv_hbm)
    for c in outs:
        c.wait()


def shards(queries, key_states, value_states, out_weight, grad_output, phases, valid_rows):
    big = lambda dtype: pltpu.VMEM((HEADS, DH, ROWS), dtype)
    dma = pltpu.SemaphoreType.DMA
    any_spec = pl.BlockSpec(memory_space=pl.ANY)
    smem = pl.BlockSpec(memory_space=pltpu.SMEM)
    chunk = (HEADS * DH // 4, D // 2)
    state = jax.ShapeDtypeStruct(queries.shape, BF16)
    near = jax.ShapeDtypeStruct((HEADS, DH, ROWS), BF16)
    shape = jax.ShapeDtypeStruct
    passed = [
        near, near, near, shape((HEADS, DH, SUB), F32), shape((2, HEADS, DH, SUB), BF16),
        shape((2, 8, HEADS, DH, SUB), BF16), shape((2, 8, HEADS, DO_ROWS, SUB), BF16), shape((2, 4, *chunk), BF16)]
    between = pl.pallas_call(
        front_kernel,
        out_shape=passed,
        in_specs=[smem, smem] + [any_spec] * 5,
        out_specs=[any_spec] * 8,
        scratch_shapes=[
            big(BF16), big(BF16), big(BF16),
            pltpu.VMEM((HEADS * DH, D), BF16), pltpu.VMEM((ROWS, D), BF16),
            big(BF16),
            pltpu.VMEM((2 * HEADS, SEG, SEG), BF16), pltpu.VMEM((SEG, SEG), BF16),
            big(F32), pltpu.VMEM((HEADS, 8, ROWS), F32), big(BF16), big(BF16),
            pltpu.VMEM((2, 2, 8, HEADS, DH, SUB), BF16),
            pltpu.VMEM((HEADS, DH, SUB), BF16), pltpu.VMEM((HEADS, DO_ROWS, SUB), BF16),
            pltpu.VMEM((HEADS, SUB, D), BF16),
            pltpu.VMEM((HEADS, SUB, SPAN), BF16), pltpu.VMEM((HEADS, DH, SUB), F32), pltpu.VMEM((HEADS, DH + 8, SUB), F32),
            big(BF16), big(BF16), big(BF16),
            pltpu.VMEM((HEADS * DH, D), F32),
            pltpu.VMEM((HEADS * DH // 2, D), BF16), pltpu.VMEM((HEADS * DH // 2, D), BF16),
            pltpu.VMEM((HEADS * DH // 2, D), F32),
            pltpu.VMEM((4, *chunk), BF16), pltpu.VMEM((4, *chunk), BF16), pltpu.VMEM((4, *chunk), BF16),
            pltpu.VMEM(chunk, BF16),
            dma((5,)), dma((3, HEADS)), dma((7,)), dma((21,)), dma((21,)), dma((28,)), dma((28,)), dma((5,)), dma((5,)),
            dma((2,)), dma((3,)), dma((3,)), dma((3,)), dma((3,)), dma((7,)), dma((7,)),
        ],
        compiler_params=pltpu.CompilerParams(
            collective_id=0, has_side_effects=True, vmem_limit_bytes=58 << 20),
        name="front",
    )(phases, valid_rows, queries, key_states, value_states, out_weight, grad_output)
    return pl.pallas_call(
        back_kernel,
        out_shape=[state, state, state, shape((HEADS * DH, D), F32)],
        in_specs=[smem, smem] + [any_spec] * 8,
        out_specs=[any_spec] * 4,
        scratch_shapes=[pltpu.VMEM(p.shape, p.dtype) for p in passed] + [
            big(BF16), big(BF16), big(BF16), pltpu.VMEM((HEADS * DH, D), F32), dma((8,)), dma((4,))],
        compiler_params=pltpu.CompilerParams(vmem_limit_bytes=58 << 20),
        name="back",
    )(phases, valid_rows, *between)


def solution(mesh):
    heads = P("dp", "tensor", None, "seq")
    return jax.shard_map(
        shards, mesh=mesh,
        in_specs=(heads, heads, heads, P("tensor", None), P("dp", "seq", None), P("tensor"), P("dp")),
        out_specs=(heads, heads, heads, P("tensor", None)),
        check_vma=False,
    )
```
